256 devices in a mesh: dp: 8 (over x, core), expert: 32 (over y, z).
Axes of the slice: x: 4, y: 4, z: 8, core: 2. Of those that a mesh axis runs over, the one named last changes fastest.
Arguments:
- tokens: bfloat16 [32768, 3072], P(('dp', 'expert')), may hold values from -24 to 24
- norm_gain: float32 [3072], replicated, may hold values from 0.1 to 1.9
- experts_chosen: int32 [32768, 4], P(('dp', 'expert')), may hold values from 0 to 31, all different within a row; in each aligned block of 128 rows (0 to 127, 128 to 255, ...) at most 18 rows name the same one
- gate_weights: float32 [32768, 4], P(('dp', 'expert')), may hold values from 0.1 to 0.6
- expert_up: bfloat16 [32, 3072, 768], P('expert'), may hold values from -0.109375 to 0.109375
- expert_down: bfloat16 [32, 768, 3072], P('expert'), may hold values from -0.21875 to 0.21875
- head_cond: bfloat16 [3072, 768], P(('dp', 'expert')), may hold values from -0.109375 to 0.109375
- head_in: bfloat16 [16, 768], replicated, may hold values from -1.5 to 1.5
- head_gain: float32 [768], replicated, may hold values from 0.1 to 1.9
- head_out: bfloat16 [16, 768], replicated, may hold values from -0.21875 to 0.21875
- latents: float32 [16, 32768], P(None, ('dp', 'expert')), may hold values from -6 to 6
- noise_draws: float32 [4, 16, 32768], P(None, None, ('dp', 'expert')), may hold values from -6 to 6
- timesteps: int32 [4, 32768], P(None, ('dp', 'expert')), may hold values from 0 to 999
Outputs:
- input_grad: bfloat16 [32768, 3072], P(('dp', 'expert'))
- cond_grad: float32 [3072, 768], P(('dp', 'expert'))
- entry_grad: float32 [16, 768], replicated
- exit_grad: float32 [16, 768], replicated
- gain_grad: float32 [768], replicated
- mean_loss: float32 [], replicated
The draws below stay inside these ranges and needn't reach their ends.
Inputs may be any that keep to these rules, and one draw needn't show every extreme that they name: `experts_chosen`: each row names 4 different experts; among the rows of one device no expert is named by more than 18 rows, a bound that some block reaches.
All inputs are finite; a program needn't handle non-finite values.
Results may differ from the reference program's by a relative error of at most 0.0095.
Values may be sent and summed in bfloat16 or wider, within the bound.
No kernel may reach another device: no remote copies, remote signals or barrier semaphores. Data moves between devices by JAX's collectives and lax.ppermute only.
A program may use at most 128 MiB of HBM per device.

```python
import math
import jax
import jax.numpy as jnp
import numpy as np
from jax import lax

D = 3072
FFW = 768
HW = 768
LAT = 16
TOPK = 4
NOISE = 4
TSTEPS = 1000
TOK_DEV = 128
EXPERTS = 32
CAP = 18
TOKENS = 32768
N_DP = 8
N_EXPERT = 32


def set_ends(drawn, own_key, low, high):
    extent = drawn.shape
    place = [jax.random.randint(jax.random.fold_in(own_key, axis), (), 0, extent[axis]) for axis in range(len(extent))]
    drawn = drawn.at[tuple(place)].set(low)
    longest = extent.index(max(extent))
    place[longest] = (place[longest] + 1) % extent[longest]
    return drawn.at[tuple(place)].set(high)


def strengthened(values, key, source, target, blocks, factor):
    def block_of(axis_at):
        return (jnp.arange(values.shape[axis_at]) // (values.shape[axis_at] // blocks)).reshape((-1,) + (1,) * (values.ndim - 1 - axis_at))

    near = jax.random.permutation(key, blocks)[block_of(target)]
    other_side = (block_of(target) + blocks // 2) % blocks
    return jnp.where((block_of(source) == near) | (block_of(source) == other_side), factor * values, values)


def steps_of(stream_key, extent, cuts, smallest, top_value):
    def one(axis_at, shards_of):
        draws = jax.random.uniform(jax.random.fold_in(jax.random.fold_in(stream_key, 6), axis_at), (shards_of,), jnp.float32, smallest / len(cuts), top_value / len(cuts))
        return jnp.repeat(jnp.exp(draws), extent[axis_at] // shards_of).reshape((-1,) + (1,) * (len(extent) - axis_at - 1))

    factor_of = one(*cuts[0])
    for cut in cuts[1:]:
        factor_of = factor_of * one(*cut)
    return factor_of


def routed_block(own_key, own, number, rows, amount, top, bound, lean):
    sequence = jax.random.permutation(own_key, amount)
    packed, ordinary = portions_of(amount, rows * top, bound, lean, True), portions_of(amount, rows * top, bound, lean, False)
    places = jnp.arange(amount)

    def named(tallies, rotation):
        used = int((tallies > 0).sum())
        fixed = max(1, used // 4)
        moved = fixed + (places - fixed + rotation * (used - fixed)) % max(1, amount - fixed)
        return jnp.zeros((amount,), jnp.int32).at[sequence[jnp.where(places < fixed, places, moved)]].set(jnp.asarray(tallies, jnp.int32))

    tallies = jnp.where(number % 4 == 0, named(packed, number // 4), named(ordinary, number - number // 4 - 1))
    mixed = jax.random.permutation(jax.random.fold_in(own, 3), amount)
    giver, taker = mixed[0:amount // 2 * 2:2], mixed[1:amount // 2 * 2:2]
    slack = jnp.minimum(tallies[giver] - 1, bound - tallies[taker]) // 2
    slack = jnp.where((giver == sequence[0]) | (taker == sequence[0]) | (tallies[taker] == 0), 0, jnp.maximum(slack, 0))
    moved = jax.random.randint(jax.random.fold_in(own, 4), (amount // 2,), 0, 1 << 20) % (slack + 1)
    tallies = tallies.at[giver].add(-moved).at[taker].add(moved)
    labels = jnp.searchsorted(jnp.cumsum(tallies), jnp.arange(rows * top), side="right").astype(jnp.int32)
    listing = labels.reshape(top, rows).T
    listing = listing[jax.random.permutation(jax.random.fold_in(own, 1), rows)]
    rotation = jax.random.randint(jax.random.fold_in(own, 2), (rows, 1), 0, top)
    return jnp.take_along_axis(listing, (jnp.arange(top)[None, :] + rotation) % top, axis=1)


def portions_of(count, total, limit, slope, full):
    portions = [(1 << 20) // math.isqrt(grade ** slope) + 1 for grade in range(1, count + 1)]
    largest = limit if full else min(limit, max(-(-total // count), total * portions[0] // sum(portions)))
    least = 1 if total - largest >= count - 1 else 0
    holding, rest = [largest] + [least] * (count - 1), total - largest - least * (count - 1)
    while rest > 0:
        free = [i for i in range(1, count) if holding[i] < largest] or [i for i in range(1, count) if holding[i] < limit]
        mass, left = sum([portions[i] for i in free]), rest
        for i in free:
            extra = min(limit - holding[i], max(1, left * portions[i] // mass), rest)
            holding[i] = holding[i] + extra
            rest = rest - extra
    return np.array(holding)


def bell_draw(key, dims, width, bound, cuts=(), kind=jnp.bfloat16):
    values = width * jax.random.normal(key, dims, jnp.float32)
    if cuts:
        values = values * steps_of(key, dims, cuts, -0.22, 0.18)
    return jnp.clip(values, -bound, bound).astype(kind)


def heavy_noise(rng, shape, width, reach, cuts, heavy, held_as=jnp.bfloat16):
    entries = width * jax.random.normal(rng, shape, jnp.float32)
    if cuts:
        entries = entries * steps_of(rng, shape, cuts, -0.22, 0.18)
    return jnp.clip(strengthened(entries, jax.random.fold_in(rng, 3), *heavy), -reach, reach).astype(held_as)


def setup_inputs(seed: int = 0) -> dict:
    key_of = jax.random.split(jax.random.key(seed), 14)
    tokens = heavy_noise(key_of[0], (TOKENS, D), 1.0, 24.0, ((0, 256),), (0, 1, 256, 6.0))
    norm_gain = jnp.clip(1.0 + 0.18 * jax.random.normal(key_of[1], (D,), jnp.float32), 0.1, 1.9)
    experts_chosen_keys = jax.random.split(jax.random.fold_in(key_of[2], 1), TOKENS // TOK_DEV)
    experts_chosen_turns = jax.random.permutation(jax.random.fold_in(key_of[2], 3), TOKENS // TOK_DEV)
    experts_chosen = jax.vmap(lambda own, number: routed_block(jax.random.fold_in(key_of[2], 2), own, number, TOK_DEV, EXPERTS, TOPK, CAP, 2))(experts_chosen_keys, experts_chosen_turns).reshape((TOKENS, TOPK))
    gate_weights = jnp.clip(0.1 + 0.5 * jax.random.uniform(key_of[3], (TOKENS, TOPK), jnp.float32) ** steps_of(key_of[3], (TOKENS, TOPK), ((0, 256),), -0.2, 0.2), 0.1, 0.6)
    expert_up = bell_draw(key_of[4], (EXPERTS, D, FFW), D ** -0.5, 0.109375, ((0, 32),))
    expert_down = bell_draw(key_of[5], (EXPERTS, FFW, D), FFW ** -0.5, 0.21875, ((0, 32),))
    head_cond = bell_draw(key_of[6], (D, HW), D ** -0.5, 0.109375, ((0, 256),))
    head_in = bell_draw(key_of[7], (LAT, HW), LAT ** -0.5, 1.5)
    head_gain = jnp.clip(1.0 + 0.18 * jax.random.normal(key_of[8], (HW,), jnp.float32), 0.1, 1.9)
    head_out = bell_draw(key_of[9], (LAT, HW), HW ** -0.5, 0.21875)
    latents = bell_draw(key_of[10], (LAT, TOKENS), 1.0, 6.0, ((1, 256),), jnp.float32)
    noise_draws = bell_draw(key_of[11], (NOISE, LAT, TOKENS), 1.0, 6.0, ((2, 256),), jnp.float32)
    timesteps = set_ends(jax.random.randint(key_of[12], (NOISE, TOKENS), 0, TSTEPS), jax.random.fold_in(key_of[12], 1), 0, TSTEPS - 1).astype(jnp.int32)
    return {"tokens": tokens, "norm_gain": norm_gain, "experts_chosen": experts_chosen, "gate_weights": gate_weights, "expert_up": expert_up, "expert_down": expert_down, "head_cond": head_cond, "head_in": head_in, "head_gain": head_gain, "head_out": head_out, "latents": latents, "noise_draws": noise_draws, "timesteps": timesteps}


NORM_EPS = 1e-06
ROOT_COEF = math.sqrt(2.0 / math.pi)
HIGH = lax.Precision.HIGHEST

def gelu_tanh(values):
    inner = ROOT_COEF * (values + 0.044715 * values * values * values)
    return 0.5 * values * (1.0 + jnp.tanh(inner))

def gelu_slope(values):
    inner = ROOT_COEF * (values + 0.044715 * values * values * values)
    tangent = jnp.tanh(inner)
    return 0.5 * (1.0 + tangent) + 0.5 * values * (1.0 - tangent * tangent) * ROOT_COEF * (1.0 + 3.0 * 0.044715 * values * values)

def signal_level(step_ids):
    fraction = (step_ids.astype(jnp.float32) / TSTEPS + 0.008) / 1.008
    cosine = jnp.cos(fraction * (math.pi / 2.0))
    return cosine * cosine

def time_embed(step_ids):
    half_width = HW // 2
    frequency = jnp.exp(-math.log(10000.0) * jnp.arange(half_width, dtype=jnp.float32) / half_width)
    angles = step_ids.astype(jnp.float32)[:, None] * frequency[None, :]
    return jnp.concatenate([jnp.cos(angles), jnp.sin(angles)], axis=1)

def head_pass(condition, head_in, head_gain, head_out, latents, noise_draws, timesteps):
    entry_f32 = head_in.astype(jnp.float32)
    exit_f32 = head_out.astype(jnp.float32)
    loss_sum = jnp.zeros((), jnp.float32)
    entry_grad = jnp.zeros_like(entry_f32)
    exit_grad = jnp.zeros_like(exit_f32)
    gain_grad = jnp.zeros_like(head_gain)
    cond_delta = jnp.zeros_like(condition)
    for draw_index in range(NOISE):
        level = signal_level(timesteps[draw_index])
        noisy = jnp.sqrt(level)[None, :] * latents + jnp.sqrt(1.0 - level)[None, :] * noise_draws[draw_index]
        entered = lax.dot_general(noisy, entry_f32, (((0,), (0,)), ((), ())), precision=HIGH)
        state = condition + entered + time_embed(timesteps[draw_index])
        centred = state - lax.optimization_barrier(jnp.mean(state, axis=1, keepdims=True))
        inv_std = lax.rsqrt(lax.optimization_barrier(jnp.mean(centred * centred, axis=1, keepdims=True)) + NORM_EPS)
        normed = centred * inv_std
        scaled = normed * head_gain
        sigmoid_val = jax.nn.sigmoid(scaled)
        active = (scaled * sigmoid_val).astype(jnp.bfloat16)
        predicted = lax.dot_general(head_out, active, (((1,), (1,)), ((), ())), preferred_element_type=jnp.float32)
        error = predicted - noise_draws[draw_index]
        loss_sum = loss_sum + jnp.sum(error * error)
        grad_pred = 2.0 / NOISE * error
        exit_grad = exit_grad + jnp.dot(grad_pred, active.astype(jnp.float32), precision=HIGH)
        grad_act = lax.dot_general(grad_pred, exit_f32, (((0,), (0,)), ((), ())), precision=HIGH)
        grad_scaled = grad_act * sigmoid_val * (1.0 + scaled * (1.0 - sigmoid_val))
        gain_grad = gain_grad + lax.optimization_barrier(jnp.sum(grad_scaled * normed, axis=0))
        grad_normed = grad_scaled * head_gain
        grad_state = inv_std * (grad_normed - lax.optimization_barrier(jnp.mean(grad_normed, axis=1, keepdims=True)) - normed * lax.optimization_barrier(jnp.mean(grad_normed * normed, axis=1, keepdims=True)))
        entry_grad = entry_grad + jnp.dot(noisy, grad_state, precision=HIGH)
        cond_delta = cond_delta + grad_state
    return (loss_sum, entry_grad, exit_grad, gain_grad, cond_delta)

def reference(tokens, norm_gain, experts_chosen, gate_weights, expert_up, expert_down, head_cond, head_in, head_gain, head_out, latents, noise_draws, timesteps):
    inputs = tokens.astype(jnp.float32)
    inverse = lax.rsqrt(lax.optimization_barrier(jnp.mean(inputs * inputs, axis=1, keepdims=True)) + NORM_EPS)
    normed_in = (inputs * inverse * norm_gain).astype(jnp.bfloat16)
    flat_expert = experts_chosen.reshape(-1).astype(jnp.int32)
    onehot = (flat_expert[:, None] == jnp.arange(EXPERTS, dtype=jnp.int32)[None, :]).astype(jnp.int32)
    running = jnp.cumsum(onehot.reshape(N_DP * N_EXPERT, TOK_DEV * TOPK, EXPERTS), axis=1).reshape(-1, EXPERTS)
    position = lax.optimization_barrier(jnp.sum(running * onehot, axis=1)) - 1
    token_of = jnp.arange(TOKENS * TOPK, dtype=jnp.int32) // TOPK
    source = token_of // TOK_DEV
    row_width = N_DP * N_EXPERT * CAP
    slot_index = flat_expert * row_width + source * CAP + position
    slot_token = jnp.full((EXPERTS * row_width,), TOKENS, jnp.int32).at[slot_index].set(token_of)
    slot_gate = jnp.zeros((EXPERTS * row_width,), jnp.float32).at[slot_index].set(gate_weights.reshape(-1))
    slot_token = slot_token.reshape(EXPERTS, row_width)
    slot_gate = slot_gate.reshape(EXPERTS, row_width)
    padded = jnp.concatenate([normed_in, jnp.zeros((1, D), jnp.bfloat16)], axis=0)

    def forward_one(mixture, pieces):
        index_row, gate_row, weight_up, weight_down = pieces
        rows_in = padded[index_row]
        pre_act = jnp.dot(rows_in, weight_up, preferred_element_type=jnp.float32)
        hidden = gelu_tanh(pre_act).astype(jnp.bfloat16)
        produced = jnp.dot(hidden, weight_down, preferred_element_type=jnp.float32).astype(jnp.bfloat16)
        mixture = mixture.at[index_row].add(produced.astype(jnp.float32) * gate_row[:, None])
        return (mixture, None)
    mixture, unused = lax.scan(forward_one, jnp.zeros((TOKENS + 1, D), jnp.float32), (slot_token, slot_gate, expert_up, expert_down))
    layer_out = (inputs + mixture[:TOKENS]).astype(jnp.bfloat16)
    condition = jnp.dot(layer_out, head_cond, preferred_element_type=jnp.float32)
    loss_sum, entry_grad, exit_grad, gain_grad, cond_delta = head_pass(condition, head_in, head_gain, head_out, latents, noise_draws, timesteps)
    delta = cond_delta.astype(jnp.bfloat16)
    grad_layer = lax.dot_general(delta, head_cond, (((1,), (1,)), ((), ())), preferred_element_type=jnp.float32)
    cond_grad = lax.dot_general(layer_out, delta, (((0,), (0,)), ((), ())), preferred_element_type=jnp.float32)
    padded_grad = jnp.concatenate([grad_layer, jnp.zeros((1, D), jnp.float32)], axis=0)

    def backward_one(collected, pieces):
        index_row, gate_row, weight_up, weight_down = pieces
        rows_in = padded[index_row]
        pre_act = jnp.dot(rows_in, weight_up, preferred_element_type=jnp.float32)
        grad_slot = (padded_grad[index_row] * gate_row[:, None]).astype(jnp.bfloat16)
        grad_hidden = lax.dot_general(grad_slot, weight_down, (((1,), (1,)), ((), ())), preferred_element_type=jnp.float32)
        grad_pre = (grad_hidden * gelu_slope(pre_act)).astype(jnp.bfloat16)
        grad_back = lax.dot_general(grad_pre, weight_up, (((1,), (1,)), ((), ())), preferred_element_type=jnp.float32).astype(jnp.bfloat16)
        collected = collected.at[index_row].add(grad_back.astype(jnp.float32))
        return (collected, None)
    collected, unused = lax.scan(backward_one, jnp.zeros((TOKENS + 1, D), jnp.float32), (slot_token, slot_gate, expert_up, expert_down))
    scaled_grad = collected[:TOKENS] * norm_gain
    grad_direct = inverse * scaled_grad - inputs * inverse * inverse * inverse * lax.optimization_barrier(jnp.mean(inputs * scaled_grad, axis=1, keepdims=True))
    input_grad = (grad_layer + grad_direct).astype(jnp.bfloat16)
    mean_loss = loss_sum / (TOKENS * NOISE)
    return (input_grad, cond_grad, entry_grad, exit_grad, gain_grad, mean_loss)
```

```python
import math

import jax
import jax.numpy as jnp
from jax import lax
from jax.sharding import Mesh, PartitionSpec as P

HW = 768
TOPK = 4
NOISE = 4
TSTEPS = 1000


NORM_EPS = 1e-06
ROOT_COEF = math.sqrt(2.0 / math.pi)
HIGH = lax.Precision.HIGHEST
CAP = 18
MAIN = 16
REST = CAP - MAIN
CORES = 2
RING = 8
DP = ("x", "core")
EXPERT = ("y", "z")
EVERY = DP + EXPERT
F32 = jnp.float32
BF16 = jnp.bfloat16


def gelu_tanh(values):
    inner = ROOT_COEF * (values + 0.044715 * values * values * values)
    return 0.5 * values * (1.0 + jnp.tanh(inner))


def gelu_slope(values):
    inner = ROOT_COEF * (values + 0.044715 * values * values * values)
    tangent = jnp.tanh(inner)
    return 0.5 * (1.0 + tangent) + 0.5 * values * (1.0 - tangent * tangent) * ROOT_COEF * (
        1.0 + 3.0 * 0.044715 * values * values
    )


def signal_level(step_ids):
    fraction = (step_ids.astype(jnp.float32) / TSTEPS + 0.008) / 1.008
    cosine = jnp.cos(fraction * (math.pi / 2.0))
    return cosine * cosine


def time_embed(step_ids):
    half_width = HW // 2
    frequency = jnp.exp(-math.log(10000.0) * jnp.arange(half_width, dtype=jnp.float32) / half_width)
    angles = step_ids.astype(jnp.float32)[:, None] * frequency[None, :]
    return jnp.concatenate([jnp.cos(angles), jnp.sin(angles)], axis=1)


def head_pass(condition, head_in, head_gain, head_out, latents, noise_draws, timesteps):
    entry_f32 = head_in.astype(jnp.float32)
    exit_f32 = head_out.astype(jnp.float32)
    loss_sum = jnp.zeros((), jnp.float32)
    entry_grad = jnp.zeros_like(entry_f32)
    exit_grad = jnp.zeros_like(exit_f32)
    gain_grad = jnp.zeros_like(head_gain)
    cond_delta = jnp.zeros_like(condition)
    for draw_index in range(NOISE):
        level = signal_level(timesteps[draw_index])
        noisy = (
            jnp.sqrt(level)[None, :] * latents
            + jnp.sqrt(1.0 - level)[None, :] * noise_draws[draw_index]
        )
        entered = lax.dot_general(noisy, entry_f32, (((0,), (0,)), ((), ())), precision=HIGH)
        state = condition + entered + time_embed(timesteps[draw_index])
        centred = state - jnp.mean(state, axis=1, keepdims=True)
        inv_std = lax.rsqrt(jnp.mean(centred * centred, axis=1, keepdims=True) + NORM_EPS)
        normed = centred * inv_std
        scaled = normed * head_gain
        sigmoid_val = jax.nn.sigmoid(scaled)
        active = (scaled * sigmoid_val).astype(jnp.bfloat16)
        predicted = lax.dot_general(
            head_out, active, (((1,), (1,)), ((), ())), preferred_element_type=jnp.float32
        )
        error = predicted - noise_draws[draw_index]
        loss_sum = loss_sum + jnp.sum(error * error)
        grad_pred = 2.0 / NOISE * error
        exit_grad = exit_grad + jnp.dot(grad_pred, active.astype(jnp.float32), precision=HIGH)
        grad_act = lax.dot_general(grad_pred, exit_f32, (((0,), (0,)), ((), ())), precision=HIGH)
        grad_scaled = grad_act * sigmoid_val * (1.0 + scaled * (1.0 - sigmoid_val))
        gain_grad = gain_grad + jnp.sum(grad_scaled * normed, axis=0)
        grad_normed = grad_scaled * head_gain
        grad_state = inv_std * (
            grad_normed
            - jnp.mean(grad_normed, axis=1, keepdims=True)
            - normed * jnp.mean(grad_normed * normed, axis=1, keepdims=True)
        )
        entry_grad = entry_grad + jnp.dot(noisy, grad_state, precision=HIGH)
        cond_delta = cond_delta + grad_state
    return (loss_sum, entry_grad, exit_grad, gain_grad, cond_delta)


def matmul(left, right, left_dim, right_dim, precision=None):
    return lax.dot_general(
        left, right, (((left_dim,), (right_dim,)), ((), ())),
        precision=precision, preferred_element_type=F32,
    )


def slot_matrix(named, before, gate_of, experts, width, first):
    lane = lax.broadcasted_iota(jnp.int32, (experts, experts * width), 1)
    row = lax.broadcasted_iota(jnp.int32, (experts, experts * width), 0)
    spread = lane // width == row
    spread_bf = spread.astype(BF16)
    place = (jnp.arange(experts * width, dtype=jnp.int32) % width + first).astype(F32)
    held = (matmul(named, spread_bf, 1, 0) > 0.5) & (matmul(before, spread_bf, 1, 0) == place)
    gates = matmul(gate_of, spread.astype(F32), 1, 0, HIGH)
    return held.astype(BF16), jnp.where(held, gates, 0.0)


def exchange(rows, experts):
    return lax.all_to_all(
        rows.reshape(experts, rows.shape[0] // experts, rows.shape[1]),
        EXPERT, split_axis=0, concat_axis=0, tiled=True,
    ).reshape(rows.shape)


def exchange_rest(rows, experts):
    width = rows.shape[1]
    packed = rows.reshape(experts, REST * width // 768, 768) if width > 768 else rows.reshape(
        experts, REST * width // 128, 128
    )
    return lax.all_to_all(packed, EXPERT, split_axis=0, concat_axis=0, tiled=True).reshape(rows.shape)


def on_device(
    tokens,
    norm_gain,
    experts_chosen,
    gate_weights,
    expert_up,
    expert_down,
    head_cond,
    head_in,
    head_gain,
    head_out,
    latents,
    noise_draws,
    timesteps,
):
    tok_rows = tokens.shape[0]
    experts = lax.axis_size(EXPERT)
    inputs = tokens.astype(F32)
    inverse = lax.rsqrt(jnp.mean(inputs * inputs, axis=1, keepdims=True) + NORM_EPS)
    normed_in = (inputs * inverse * norm_gain).astype(BF16)

    chosen = experts_chosen[:, :, None] == jnp.arange(experts, dtype=jnp.int32)[None, None, :]
    named = jnp.any(chosen, axis=1).astype(BF16)
    gate_of = jnp.sum(jnp.where(chosen, gate_weights[:, :, None], 0.0), axis=1)
    earlier = jnp.tril(jnp.ones((tok_rows, tok_rows), BF16), -1)
    before = matmul(earlier, named, 1, 0).astype(BF16)
    pick, gate = slot_matrix(named, before, gate_of, experts, MAIN, 0)
    pick_rest, gate_rest = slot_matrix(named, before, gate_of, experts, REST, MAIN)
    slot_gate = jnp.sum(gate, axis=0)[:, None]
    slot_gate_rest = jnp.sum(gate_rest, axis=0)[:, None]

    cond_part = lax.all_gather(head_cond.reshape(-1, 128), EXPERT, axis=0, tiled=True)
    cond_full = lax.all_gather(cond_part.reshape(-1, HW), DP, axis=0, tiled=True)

    weight_up = expert_up[0]
    weight_down = expert_down[0]
    rows = exchange(matmul(pick, normed_in, 0, 0).astype(BF16), experts)
    rows_rest = exchange_rest(matmul(pick_rest, normed_in, 0, 0).astype(BF16), experts)
    down_cond = matmul(weight_down, cond_full, 1, 0).astype(BF16)
    direct_condition = matmul(tokens, cond_full, 1, 0)

    pre_act = matmul(rows, weight_up, 1, 0)
    pre_act_rest = matmul(rows_rest, weight_up, 1, 0)
    hidden = gelu_tanh(pre_act).astype(BF16)
    hidden_rest = gelu_tanh(pre_act_rest).astype(BF16)
    added = exchange(matmul(hidden, down_cond, 1, 0).astype(BF16), experts)
    added_rest = exchange_rest(matmul(hidden_rest, down_cond, 1, 0).astype(BF16), experts)
    condition = (
        direct_condition
        + matmul(gate, added.astype(F32), 1, 0, HIGH)
        + matmul(gate_rest, added_rest.astype(F32), 1, 0, HIGH)
    )

    loss_sum, entry_grad, exit_grad, gain_grad, cond_delta = head_pass(
        condition, head_in, head_gain, head_out, latents, noise_draws, timesteps
    )
    delta = cond_delta.astype(BF16)
    grads = exchange((matmul(pick, delta, 0, 0) * slot_gate).astype(BF16), experts)
    grads_rest = exchange_rest((matmul(pick_rest, delta, 0, 0) * slot_gate_rest).astype(BF16), experts)
    grad_layer = matmul(delta, cond_full, 1, 1)
    direct_cond_grad = matmul(tokens, delta, 0, 0)

    grad_pre = (matmul(grads, down_cond, 1, 1) * gelu_slope(pre_act)).astype(BF16)
    grad_pre_rest = (matmul(grads_rest, down_cond, 1, 1) * gelu_slope(pre_act_rest)).astype(BF16)
    back = exchange(matmul(grad_pre, weight_up, 1, 1).astype(BF16), experts)
    back_rest = exchange_rest(matmul(grad_pre_rest, weight_up, 1, 1).astype(BF16), experts)

    hidden_grads = matmul(hidden, grads, 0, 0) + matmul(hidden_rest, grads_rest, 0, 0)
    cond_grad = direct_cond_grad + matmul(weight_down, hidden_grads.astype(BF16), 0, 0)
    cond_grad = lax.psum_scatter(cond_grad, DP, scatter_dimension=0, tiled=True)
    cond_grad = lax.all_to_all(
        cond_grad.reshape(experts, -1, 128).astype(BF16), EXPERT, split_axis=0, concat_axis=0, tiled=True
    )
    cond_grad = jnp.sum(cond_grad.astype(F32), axis=0).reshape(-1, HW)
    loss_sum, entry_grad, exit_grad, gain_grad = lax.psum(
        (loss_sum, entry_grad, exit_grad, gain_grad), EVERY
    )

    grad_normed = matmul(pick, back, 1, 0) + matmul(pick_rest, back_rest, 1, 0)
    scaled_grad = grad_normed * norm_gain
    grad_direct = inverse * scaled_grad - inputs * inverse * inverse * inverse * jnp.mean(
        inputs * scaled_grad, axis=1, keepdims=True
    )
    input_grad = (grad_layer + grad_direct).astype(BF16)
    mean_loss = loss_sum / (tok_rows * lax.axis_size(EVERY) * NOISE)
    return (input_grad, cond_grad, entry_grad, exit_grad, gain_grad, mean_loss)


def solution(mesh):
    shape = (mesh.shape["dp"] // CORES, CORES, mesh.shape["expert"] // RING, RING)
    fine = Mesh(mesh.devices.reshape(shape), EVERY)
    return jax.shard_map(
        on_device,
        mesh=fine,
        in_specs=(
            P(EVERY, None),
            P(),
            P(EVERY, None),
            P(EVERY, None),
            P(EXPERT, None, None),
            P(EXPERT, None, None),
            P(EVERY, None),
            P(),
            P(),
            P(),
            P(None, EVERY),
            P(None, None, EVERY),
            P(None, EVERY),
        ),
        out_specs=(P(EVERY, None), P(EVERY, None), P(), P(), P(), P()),
        check_vma=False,
    )
```

```python
import math

import jax
import jax.numpy as jnp
from jax import lax
from jax.experimental import pallas as pl
from jax.experimental.pallas import tpu as pltpu
from jax.sharding import Mesh, PartitionSpec as P

HW = 768
TOPK = 4
NOISE = 4
TSTEPS = 1000


NORM_EPS = 1e-06
ROOT_COEF = math.sqrt(2.0 / math.pi)
HIGH = lax.Precision.HIGHEST
DP = ("x", "core")
EXPERT = ("y", "z")
EVERY = DP + EXPERT
CORES = 2
RING = 8
F32 = jnp.float32
BF16 = jnp.bfloat16

MAIN = 16
REST = 8
WIDE = 4
LESS_PART = 256
MORE_PART = 512
HALF_PART = 384
TAIL = 40
NARROW = 3
NARROW_PART = 256
LANES = 128
ENTRY_ROW = 0
EXIT_ROW = 96
GAIN_ROW = 192
LOSS_ROW = 198


def gelu_tanh(values):
    inner = ROOT_COEF * (values + 0.044715 * values * values * values)
    return 0.5 * values * (1.0 + jnp.tanh(inner))


def gelu_slope(values):
    inner = ROOT_COEF * (values + 0.044715 * values * values * values)
    tangent = jnp.tanh(inner)
    return 0.5 * (1.0 + tangent) + 0.5 * values * (1.0 - tangent * tangent) * ROOT_COEF * (
        1.0 + 3.0 * 0.044715 * values * values
    )


def signal_level(step_ids):
    fraction = (step_ids.astype(jnp.float32) / TSTEPS + 0.008) / 1.008
    cosine = jnp.cos(fraction * (math.pi / 2.0))
    return cosine * cosine


def time_embed(step_ids):
    half_width = HW // 2
    frequency = jnp.exp(-math.log(10000.0) * jnp.arange(half_width, dtype=jnp.float32) / half_width)
    angles = step_ids.astype(jnp.float32)[:, None] * frequency[None, :]
    return jnp.concatenate([jnp.cos(angles), jnp.sin(angles)], axis=1)


def matmul(left, right, left_dim=1, right_dim=0, precision=None):
    return lax.dot_general(
        left, right, (((left_dim,), (right_dim,)), ((), ())),
        precision=precision, preferred_element_type=F32,
    )


def iota(shape, axis):
    return lax.broadcasted_iota(jnp.int32, shape, axis)


def of_part(rows, part):
    return ((iota((rows, 1), 0) & 7) >> 1) == part


def rest_rows(peers, part):
    row, col = iota((peers * 2, peers * REST), 0), iota((peers * 2, peers * REST), 1)
    return jnp.where(col == (row >> 1) * REST + part * 2 + (row & 1), 1.0, 0.0).astype(BF16)


def rest_spread(peers, part):
    row, col = iota((peers * REST, peers * 2), 0), iota((peers * REST, peers * 2), 1)
    return jnp.where(row == (col >> 1) * REST + part * 2 + (col & 1), 1.0, 0.0).astype(BF16)


def bring(sources, targets, sems):
    copies = [pltpu.make_async_copy(*ends, sems.at[i]) for i, ends in enumerate(zip(sources, targets))]
    for copy in copies:
        copy.start()
    return copies


def flat(block):
    return block.reshape(block.shape[0] * block.shape[1], block.shape[2])


def main_of(block, part):
    return flat(block[:, MAIN * part : MAIN * (part + 1), :])


def rest_of(block, parts):
    return flat(block[:, MAIN * parts : MAIN * parts + REST, :].astype(F32)).astype(BF16)


def dispatch_kernel(
    tokens_in, gain_in, chosen_in, gates_in, cond_in, send_ref, later_ref, gate_ref, inverse_ref,
    normed_ref, tokens_ref, gain_ref, chosen_ref, gates_ref, cond_ref, own_ref, sems,
):
    step = pl.program_id(0)
    tok_rows = tokens_ref.shape[0]
    experts = gate_ref.shape[0] // (MAIN + REST)
    group = send_ref.shape[0]
    main_rows = experts * MAIN

    @pl.when(step == 0)
    def _():
        sources = (tokens_in, gain_in, chosen_in, gates_in, cond_in)
        for copy in bring(sources, (tokens_ref, gain_ref, chosen_ref, gates_ref, cond_ref), sems):
            copy.wait()
        own_ref[...] = jnp.zeros_like(own_ref)
        cond = cond_ref[...].astype(F32)
        cond_rows = cond.shape[0]
        for piece in range(NARROW):
            columns = slice(piece * NARROW_PART, (piece + 1) * NARROW_PART)
            own_ref[piece * cond_rows : (piece + 1) * cond_rows, :] = cond[:, columns]
        inputs = tokens_ref[...].astype(F32)
        inverse = lax.rsqrt(jnp.mean(inputs * inputs, axis=1, keepdims=True) + NORM_EPS)
        inverse_ref[...] = inverse
        normed_ref[...] = (inputs * inverse * gain_ref[...]).astype(BF16)
        ids = iota((experts, tok_rows), 0)
        named = jnp.zeros((experts, tok_rows), F32)
        gate_of = jnp.zeros((experts, tok_rows), F32)
        for choice in range(TOPK):
            hit = chosen_ref[choice : choice + 1, :] == ids
            named = named + jnp.where(hit, 1.0, 0.0)
            gate_of = gate_of + jnp.where(hit, gates_ref[choice : choice + 1, :], 0.0)
        earlier = jnp.where(iota((tok_rows, tok_rows), 0) < iota((tok_rows, tok_rows), 1), 1.0, 0.0)
        named = named.astype(BF16)
        before = matmul(named, earlier.astype(BF16)).astype(BF16)

        def slots(first, rows, shift, slot):
            spread = jnp.where((iota((rows, experts), 0) >> shift) == iota((rows, experts), 1), 1.0, 0.0)
            spread_bf = spread.astype(BF16)
            held = (matmul(spread_bf, named) > 0.5) & (matmul(spread_bf, before) == slot.astype(F32))
            gates = matmul(spread, gate_of, precision=HIGH)
            gate_ref[first : first + rows, :] = jnp.where(held, gates, 0.0)

        slots(0, main_rows, 4, iota((main_rows, tok_rows), 0) & 15)
        rows = experts * REST
        slots(main_rows, rows, 3, 16 + (iota((rows, tok_rows), 0) & 1))

    main_at = pl.multiple_of(step * (group * MAIN), group * MAIN)
    rest_at = pl.multiple_of(main_rows + step * (group * REST), group * REST)
    pick = jnp.where(gate_ref[pl.ds(main_at, group * MAIN), :] != 0.0, 1.0, 0.0).astype(BF16)
    rest = jnp.where(gate_ref[pl.ds(rest_at, group * REST), :] != 0.0, 1.0, 0.0)
    first = 0
    for out_ref in (send_ref, later_ref):
        width = out_ref.shape[2]
        total = jnp.zeros((group * REST, width), F32)
        for part in range(WIDE):
            piece = normed_ref[:, first : first + width]
            first = first + width
            main = matmul(pick, piece).astype(BF16)
            out_ref[:, MAIN * part : MAIN * (part + 1), :] = main.reshape(group, MAIN, width)
            total = total + matmul(jnp.where(of_part(group * REST, part), rest, 0.0).astype(BF16), piece)
        tail = total.reshape(group, REST, width)
        if out_ref is send_ref:
            own = jnp.broadcast_to(own_ref[...][None], (group,) + own_ref.shape)
            tail = jnp.concatenate([tail, own], axis=1)
        out_ref[:, MAIN * WIDE :, :] = tail.astype(BF16)


def gather_rows(rows_ref, held_ref, part, column):
    peers = rows_ref.shape[0]
    main_rows = peers * MAIN
    main = rows_ref[:, pl.ds(pl.multiple_of(part * MAIN, MAIN), MAIN), :]
    columns = slice(column, column + rows_ref.shape[2])
    held_ref[:main_rows, columns] = flat(main)
    held_ref[main_rows:, columns] = matmul(rest_rows(peers, part), rest_of(rows_ref, WIDE)).astype(BF16)


def first_kernel(rows_ref, up_ref, pre_ref, held_ref):
    step = pl.program_id(0)
    gather_rows(rows_ref, held_ref, 2 * step, 0)
    gather_rows(rows_ref, held_ref, 2 * step + 1, rows_ref.shape[2])
    product = matmul(held_ref[...], up_ref[...])

    @pl.when(step == 0)
    def _():
        pre_ref[...] = product

    @pl.when(step > 0)
    def _():
        pre_ref[...] += product


def forward_kernel(
    rows_ref, up_ref, start_in, mixed_in, pre_ref, hidden_ref, send_ref, held_ref, start_ref, mixed_ref, sems
):
    step = pl.program_id(0)
    start_copy = pltpu.make_async_copy(start_in, start_ref, sems.at[0])
    mixed_copy = pltpu.make_async_copy(mixed_in, mixed_ref, sems.at[1])

    @pl.when(step == 0)
    def _():
        start_copy.start()
        mixed_copy.start()

    peers = rows_ref.shape[0]
    main_rows = peers * MAIN
    gather_rows(rows_ref, held_ref, 2 * step, 0)
    gather_rows(rows_ref, held_ref, 2 * step + 1, rows_ref.shape[2])
    product = matmul(held_ref[...], up_ref[...])

    @pl.when(step == 0)
    def _():
        start_copy.wait()
        pre_ref[...] = start_ref[...] + product

    @pl.when(step == WIDE // 2 - 1)
    def _():
        pre_act = pre_ref[...] + product
        pre_ref[...] = pre_act
        hidden = gelu_tanh(pre_act).astype(BF16)
        hidden_ref[...] = hidden
        mixed_copy.wait()
        added = matmul(hidden, mixed_ref[...]).astype(BF16)
        total = jnp.zeros((peers * REST, NARROW_PART), F32)
        for piece in range(NARROW):
            columns = slice(piece * NARROW_PART, (piece + 1) * NARROW_PART)
            send_ref[:, MAIN * piece : MAIN * (piece + 1), :] = added[:main_rows, columns].reshape(
                peers, MAIN, NARROW_PART
            )
            total = total + matmul(rest_spread(peers, piece), added[main_rows:, columns])
        send_ref[:, MAIN * NARROW :, :] = total.reshape(peers, REST, NARROW_PART).astype(BF16)


def two(values):
    high = values.astype(BF16).astype(F32)
    return jnp.concatenate([high, values - high], axis=values.ndim - 1)


def head_kernel(
    added_ref, direct_ref, offset_in, noisy_ref, noise_in, gain_ref, out_in, gate_in,
    delta_ref, send_ref, condition_ref, small_ref, offset_ref, noise_ref, out_ref, gate_ref, sems,
):
    copies = bring((gate_in, offset_in, noise_in, out_in), (gate_ref, offset_ref, noise_ref, out_ref), sems)
    copies[0].wait()
    peers = added_ref.shape[0]
    main_rows = peers * MAIN
    gate, gate_rest = gate_ref[:main_rows, :], gate_ref[main_rows:, :]
    rest = rest_of(added_ref, NARROW).astype(F32)
    for piece in range(NARROW):
        columns = slice(piece * NARROW_PART, (piece + 1) * NARROW_PART)
        mine = jnp.where(of_part(peers * REST, piece), gate_rest, 0.0)
        condition_ref[:, columns] = (
            direct_ref[:, columns]
            + matmul(gate, main_of(added_ref, piece).astype(F32), 0, 0, HIGH)
            + matmul(mine, rest, 0, 0, HIGH)
        )
    for copy in copies[1:]:
        copy.wait()
    condition = condition_ref[...]
    gain = gain_ref[...]
    head_out = out_ref[...]
    exit_f32 = head_out.astype(F32)
    loss = jnp.zeros((1, 1), F32)
    entry_grad = jnp.zeros_like(exit_f32)
    exit_grad = jnp.zeros_like(exit_f32)
    gain_grad = jnp.zeros_like(gain)
    cond_delta = jnp.zeros_like(condition)
    for draw in range(NOISE):
        state = condition + offset_ref[draw]
        centred = state - jnp.mean(state, axis=1, keepdims=True)
        inv_std = lax.rsqrt(jnp.mean(centred * centred, axis=1, keepdims=True) + NORM_EPS)
        normed = centred * inv_std
        scaled = normed * gain
        sigmoid_val = 1.0 / (1.0 + jnp.exp(-scaled))
        active = (scaled * sigmoid_val).astype(BF16)
        error = matmul(head_out, active, 1, 1) - noise_ref[draw]
        loss = loss + jnp.sum(jnp.sum(error * error, axis=1, keepdims=True), axis=0, keepdims=True)
        grad_pred = 2.0 / NOISE * error
        exit_grad = exit_grad + matmul(grad_pred, active.astype(F32), 1, 0, HIGH)
        grad_act = matmul(grad_pred, exit_f32, 0, 0, HIGH)
        grad_scaled = grad_act * sigmoid_val * (1.0 + scaled * (1.0 - sigmoid_val))
        gain_grad = gain_grad + jnp.sum(grad_scaled * normed, axis=0, keepdims=True)
        grad_normed = grad_scaled * gain
        grad_state = inv_std * (
            grad_normed
            - jnp.mean(grad_normed, axis=1, keepdims=True)
            - normed * jnp.mean(grad_normed * normed, axis=1, keepdims=True)
        )
        entry_grad = entry_grad + matmul(noisy_ref[draw], grad_state, 1, 0, HIGH)
        cond_delta = cond_delta + grad_state
    delta = cond_delta.astype(BF16)
    delta_ref[...] = delta

    small_ref[...] = jnp.zeros_like(small_ref)
    channels = entry_grad.shape[0]
    for block in range(HW // LANES):
        columns = slice(block * LANES, (block + 1) * LANES)
        at = block * channels
        small_ref[ENTRY_ROW + at : ENTRY_ROW + at + channels, :] = entry_grad[:, columns]
        small_ref[EXIT_ROW + at : EXIT_ROW + at + channels, :] = exit_grad[:, columns]
        small_ref[GAIN_ROW + block : GAIN_ROW + block + 1, :] = gain_grad[:, columns]
    small_ref[LOSS_ROW : LOSS_ROW + 1, :] = jnp.broadcast_to(loss, (1, LANES))
    small = two(small_ref[...].reshape(peers, small_ref.shape[0] // peers, LANES))

    pick = jnp.where(gate != 0.0, 1.0, 0.0).astype(BF16)
    pick_rest = jnp.where(gate_rest != 0.0, 1.0, 0.0)
    slot_gate = jnp.sum(gate, axis=1, keepdims=True)
    total = jnp.zeros((peers * REST, NARROW_PART), F32)
    for piece in range(NARROW):
        columns = delta[:, piece * NARROW_PART : (piece + 1) * NARROW_PART]
        main = (matmul(pick, columns) * slot_gate).astype(BF16)
        send_ref[:, MAIN * piece : MAIN * (piece + 1), :] = main.reshape(peers, MAIN, NARROW_PART)
        mine = jnp.where(of_part(peers * REST, piece), pick_rest, 0.0).astype(BF16)
        total = total + matmul(mine, columns)
    total = total * jnp.sum(gate_rest, axis=1, keepdims=True)
    tail = jnp.concatenate([total.reshape(peers, REST, NARROW_PART), small], axis=1)
    send_ref[:, MAIN * NARROW :, :] = tail.astype(BF16)


def send_back(held_ref, up_ref, send_ref, rest_ref):
    step = pl.program_id(0)
    peers = send_ref.shape[0]
    main_rows = peers * MAIN
    back = matmul(held_ref[...], up_ref[...], 1, 1).astype(BF16)

    @pl.when(step == 0)
    def _():
        rest_ref[...] = jnp.zeros_like(rest_ref)

    width = send_ref.shape[2]
    for side in range(2):
        part = 2 * step + side
        columns = slice(side * width, (side + 1) * width)
        send_ref[:, pl.ds(pl.multiple_of(part * MAIN, MAIN), MAIN), :] = back[:main_rows, columns].reshape(
            peers, MAIN, width
        )
        rest_ref[...] += matmul(rest_spread(peers, part), back[main_rows:, columns])

    @pl.when(step == WIDE // 2 - 1)
    def _():
        send_ref[:, MAIN * WIDE :, :] = rest_ref[...].reshape(peers, REST, width).astype(BF16)


def backward_kernel(
    grads_ref, mixed_in, slope_ref, up_ref, slot_ref, held_ref, small_ref, send_ref, rest_ref, mixed_ref, sem
):
    peers = grads_ref.shape[0]
    main_rows = peers * MAIN

    @pl.when(pl.program_id(0) == 0)
    def _():
        mixed_copy = pltpu.make_async_copy(mixed_in, mixed_ref, sem)
        mixed_copy.start()
        tail = grads_ref[:, MAIN * NARROW :, :].astype(F32)
        rest = flat(tail[:, :REST, :]).astype(BF16)
        for piece in range(NARROW):
            columns = slice(piece * NARROW_PART, (piece + 1) * NARROW_PART)
            slot_ref[:main_rows, columns] = main_of(grads_ref, piece)
            slot_ref[main_rows:, columns] = matmul(rest_rows(peers, piece), rest).astype(BF16)
        mixed_copy.wait()
        grad_hidden = matmul(slot_ref[...], mixed_ref[...], 1, 1)
        held_ref[...] = (grad_hidden * slope_ref[...]).astype(BF16)
        small = jnp.sum(tail[:, REST:, :], axis=0)
        small_ref[...] = small[:, :LANES] + small[:, LANES:]

    send_back(held_ref, up_ref, send_ref, rest_ref)


def second_kernel(held_ref, up_ref, send_ref, rest_ref):
    send_back(held_ref, up_ref, send_ref, rest_ref)


def cond_grad_kernel(slot_ref, hidden_ref, delta_ref, down_ref, tokens_ref, grad_ref, both_ref, delta_t_ref):
    @pl.when(pl.program_id(0) == 0)
    def _():
        both_ref[...] = matmul(slot_ref[...], hidden_ref[...], 0, 0).astype(BF16)
        delta_t_ref[...] = delta_ref[...].astype(F32).T.astype(BF16)

    total = matmul(both_ref[...], down_ref[...]) + matmul(delta_t_ref[...], tokens_ref[...])
    width = grad_ref.shape[2]
    for side in range(grad_ref.shape[0]):
        grad_ref[side] = total[:, side * width : (side + 1) * width]


def grad_part(block_ref, gate_ref, tokens_ref, gain_ref, scaled_ref, first, mean):
    peers = block_ref.shape[0]
    main_rows = peers * MAIN
    pick = jnp.where(gate_ref[:main_rows, :] != 0.0, 1.0, 0.0).astype(BF16)
    pick_rest = jnp.where(gate_ref[main_rows:, :] != 0.0, 1.0, 0.0)
    rest = rest_of(block_ref, WIDE)
    width = block_ref.shape[2]
    for part in range(WIDE):
        here = slice(part * width, (part + 1) * width)
        columns = slice(first + part * width, first + (part + 1) * width)
        mine = jnp.where(of_part(peers * REST, part), pick_rest, 0.0).astype(BF16)
        total = matmul(pick, main_of(block_ref, part), 0, 0) + matmul(mine, rest, 0, 0)
        scaled = total * gain_ref[:, columns]
        scaled_ref[:, here] = scaled
        mean = mean + jnp.sum(tokens_ref[:, columns].astype(F32) * scaled, axis=1, keepdims=True)
    return mean


def front_kernel(block_ref, gate_ref, tokens_ref, gain_ref, scaled_ref, mean_ref):
    mean_ref[...] = grad_part(block_ref, gate_ref, tokens_ref, gain_ref, scaled_ref, 0, jnp.zeros_like(mean_ref))


def finish_kernel(
    block_ref, front_ref, mean_ref, gate_ref, layer_ref, tokens_ref, inverse_ref, gain_ref, grad_ref, scaled_ref
):
    half = front_ref.shape[1]
    mean = grad_part(block_ref, gate_ref, tokens_ref, gain_ref, scaled_ref, half, mean_ref[...])
    mean = mean / tokens_ref.shape[1]
    inverse = inverse_ref[...]
    cubed = inverse * inverse * inverse * mean
    first = 0
    for part_ref in (front_ref, scaled_ref):
        columns = slice(first, first + part_ref.shape[1])
        first = first + part_ref.shape[1]
        direct = inverse * part_ref[...] - tokens_ref[:, columns].astype(F32) * cubed
        grad_ref[:, columns] = (layer_ref[:, columns] + direct).astype(BF16)


def totals_kernel(sums_ref, cond_ref, entry_ref, exit_ref, gain_ref, loss_ref, total_ref, small_ref):
    dense = total_ref.shape[0]
    peers = sums_ref.shape[0]
    total_ref[...] = jnp.sum(sums_ref[:, :dense, :].astype(F32), axis=0)
    blocks = cond_ref.shape[1] // LANES
    for block in range(blocks):
        cond_ref[:, block * LANES : (block + 1) * LANES] = total_ref[pl.ds(block, dense // blocks, stride=blocks), :]
    small = sums_ref[:, dense:, :].astype(F32)
    small_ref[...] = flat(small[:, :8, :] + small[:, 8:, :])
    channels = entry_ref.shape[0]
    for block in range(blocks):
        columns = slice(block * LANES, (block + 1) * LANES)
        at = block * channels
        entry_ref[:, columns] = small_ref[ENTRY_ROW + at : ENTRY_ROW + at + channels, :]
        exit_ref[:, columns] = small_ref[EXIT_ROW + at : EXIT_ROW + at + channels, :]
        gain_ref[:, columns] = small_ref[GAIN_ROW + block : GAIN_ROW + block + 1, :]
    loss_ref[...] = small_ref[LOSS_ROW : LOSS_ROW + 1, :]


def whole(*shape):
    return pl.BlockSpec(shape, lambda *step: (0,) * len(shape))


def once(*shape):
    return pl.BlockSpec(shape, lambda *step: (0,) * len(shape), pipeline_mode=pl.Buffered(1))


def stored(shape, dtype):
    return pltpu.HBM(shape, dtype)


def shaped(shape, dtype):
    return jax.ShapeDtypeStruct(shape, dtype)


def call(kernel, grid, in_specs, out_specs, out_shape, scratch, flops, moved):
    return pl.pallas_call(
        kernel,
        grid=grid,
        in_specs=in_specs,
        out_specs=out_specs,
        out_shape=out_shape,
        scratch_shapes=scratch,
        compiler_params=pltpu.CompilerParams(vmem_limit_bytes=48 << 20),
        cost_estimate=pl.CostEstimate(flops=flops, bytes_accessed=moved, transcendentals=0),
    )


def exchange(block):
    return lax.all_to_all(block, EXPERT, split_axis=0, concat_axis=0, tiled=True)


def on_device(
    tokens,
    norm_gain,
    experts_chosen,
    gate_weights,
    expert_up,
    expert_down,
    head_cond,
    head_in,
    head_gain,
    head_out,
    latents,
    noise_draws,
    timesteps,
):
    tok_rows, width = tokens.shape
    experts = lax.axis_size(EXPERT)
    features = expert_up.shape[2]
    rows = experts * (MAIN + 2)
    slot_rows = experts * (MAIN + REST)
    less, more = LESS_PART, MORE_PART
    block_rows = WIDE * MAIN + REST
    less_block, more_block = (experts, block_rows, less), (experts, block_rows, more)
    cond_rows = head_cond.shape[0]
    joined = less_block[:1] + (block_rows + TAIL, less)
    half = HALF_PART
    half_block = (experts, block_rows, half)
    narrow_block = (experts, NARROW * MAIN + REST, NARROW_PART)
    grads_block = (experts, NARROW * MAIN + REST + 8, NARROW_PART)
    small_rows = 8
    steps = WIDE // 2
    group = 8
    gain_row = norm_gain.reshape(1, width)
    far = pl.BlockSpec(memory_space=pltpu.HBM)
    weight_up = expert_up[0]
    weight_down = expert_down[0]
    expert_flops = rows * features * width

    send, send_later, gate, inverse = call(
        dispatch_kernel,
        (experts // group,),
        [far, far, far, far, far],
        [
            pl.BlockSpec((group,) + joined[1:], lambda step: (step, 0, 0)),
            pl.BlockSpec((group,) + more_block[1:], lambda step: (step, 0, 0)),
            whole(slot_rows, tok_rows),
            whole(tok_rows, 1),
        ],
        [
            stored(joined, BF16),
            stored(more_block, BF16),
            stored((slot_rows, tok_rows), F32),
            stored((tok_rows, 1), F32),
        ],
        [
            pltpu.VMEM((tok_rows, width), BF16),
            pltpu.VMEM((tok_rows, width), BF16),
            pltpu.VMEM((1, width), F32),
            pltpu.VMEM((TOPK, tok_rows), jnp.int32),
            pltpu.VMEM((TOPK, tok_rows), F32),
            pltpu.VMEM(head_cond.shape, BF16),
            pltpu.VMEM((TAIL, less), F32),
            pltpu.SemaphoreType.DMA((5,)),
        ],
        800_000_000,
        5_000_000,
    )(tokens, gain_row, experts_chosen.T, gate_weights.T, head_cond)

    def of_draws():
        levels = signal_level(timesteps)[:, None, :]
        noisy = jnp.sqrt(levels) * latents[None] + jnp.sqrt(1.0 - levels) * noise_draws
        entered = lax.dot_general(noisy, head_in.astype(F32), (((1,), (0,)), ((), ())), precision=HIGH)
        return entered + time_embed(timesteps.reshape(-1)).reshape(NOISE, tok_rows, HW), noisy

    core = lax.axis_index("core")
    shapes = ((NOISE, tok_rows, HW), noise_draws.shape)
    early = lax.cond(core == 0, of_draws, lambda: tuple(jnp.zeros(shape, F32) for shape in shapes))

    send, early = lax.optimization_barrier((send, early))
    arrived = exchange(send)
    arrived_later = exchange(send_later)
    cond_part = arrived[:, block_rows : block_rows + NARROW * cond_rows, :]
    cond_part = cond_part.reshape(experts, NARROW, cond_rows, NARROW_PART).transpose(0, 2, 1, 3).reshape(-1, HW)
    cond_full = lax.all_gather(cond_part, DP, axis=0, tiled=True)

    down_cond = matmul(weight_down, cond_full).astype(BF16)
    direct = matmul(tokens, cond_full)

    pre_act = call(
        first_kernel,
        (steps,),
        [once(*joined), pl.BlockSpec((2 * less, features), lambda step: (step, 0))],
        whole(rows, features),
        stored((rows, features), F32),
        [pltpu.VMEM((rows, 2 * less), BF16)],
        expert_flops,
        6_000_000,
    )(arrived, weight_up)
    pre_act, hidden, send = call(
        forward_kernel,
        (steps,),
        [
            once(*more_block),
            pl.BlockSpec((2 * more, features), lambda step: (step + 1, 0)),
            far,
            far,
        ],
        [whole(rows, features), whole(rows, features), whole(*narrow_block)],
        [stored((rows, features), F32), stored((rows, features), BF16), stored(narrow_block, BF16)],
        [
            pltpu.VMEM((rows, 2 * more), BF16),
            pltpu.VMEM((rows, features), F32),
            pltpu.VMEM((features, HW), BF16),
            pltpu.SemaphoreType.DMA((2,)),
        ],
        2 * expert_flops,
        10_000_000,
    )(arrived_later, weight_up, pre_act, down_cond)
    added = exchange(send)
    offset, noisy = lax.cond(core == 1, of_draws, lambda: early)
    slope = gelu_slope(pre_act)

    delta, send = call(
        head_kernel,
        (1,),
        [
            whole(*narrow_block),
            whole(tok_rows, HW),
            far,
            whole(*noisy.shape),
            far,
            whole(1, HW),
            far,
            far,
        ],
        [whole(tok_rows, HW), whole(*grads_block)],
        [stored((tok_rows, HW), BF16), stored(grads_block, BF16)],
        [
            pltpu.VMEM((tok_rows, HW), F32),
            pltpu.VMEM((experts * small_rows, LANES), F32),
            pltpu.VMEM((NOISE, tok_rows, HW), F32),
            pltpu.VMEM(noise_draws.shape, F32),
            pltpu.VMEM(head_out.shape, BF16),
            pltpu.VMEM((slot_rows, tok_rows), F32),
            pltpu.SemaphoreType.DMA((4,)),
        ],
        1_500_000_000,
        5_000_000,
    )(added, direct, offset, noisy, noise_draws, head_gain.reshape(1, HW), head_out, gate)
    arrived = exchange(send)

    slot_grads, held, small, send = call(
        backward_kernel,
        (steps,),
        [
            once(*grads_block),
            far,
            once(rows, features),
            pl.BlockSpec((2 * half, features), lambda step: (step, 0)),
        ],
        [whole(rows, HW), whole(rows, features), whole(small_rows, LANES), whole(*half_block)],
        [
            stored((rows, HW), BF16),
            stored((rows, features), BF16),
            stored((small_rows, LANES), F32),
            stored(half_block, BF16),
        ],
        [
            pltpu.VMEM((experts * REST, half), F32),
            pltpu.VMEM((features, HW), BF16),
            pltpu.SemaphoreType.DMA,
        ],
        2 * expert_flops,
        10_000_000,
    )(arrived, down_cond, slope, weight_up)
    slot_grads, held, small, send = lax.optimization_barrier((slot_grads, held, small, send))
    front = exchange(send)
    send = call(
        second_kernel,
        (steps,),
        [once(rows, features), pl.BlockSpec((2 * half, features), lambda step: (step + steps, 0))],
        whole(*half_block),
        stored(half_block, BF16),
        [pltpu.VMEM((experts * REST, half), F32)],
        0,
        0,
    )(held, weight_up)

    back = exchange(send)

    chunks = lax.axis_size(DP)
    chunk = width // chunks
    cond_grad = call(
        cond_grad_kernel,
        (chunks // 2,),
        [
            once(rows, HW),
            once(rows, features),
            once(tok_rows, HW),
            pl.BlockSpec((features, 2 * chunk), lambda step: (0, step)),
            pl.BlockSpec((tok_rows, 2 * chunk), lambda step: (0, step)),
        ],
        pl.BlockSpec((2, HW, chunk), lambda step: (step, 0, 0)),
        stored((chunks, HW, chunk), F32),
        [pltpu.VMEM((HW, features), BF16), pltpu.VMEM((HW, tok_rows), BF16)],
        0,
        0,
    )(slot_grads, hidden, delta, weight_down, tokens)
    cond_grad = lax.psum_scatter(cond_grad, DP, scatter_dimension=0, tiled=True)[0]
    small, front = lax.optimization_barrier((small, front))
    small = lax.all_gather(small, DP, axis=0, tiled=True)
    small = jnp.sum(small.reshape(-1, small_rows, LANES), axis=0)
    high = lax.reduce_precision(small, 8, 7)
    small = jnp.concatenate([high, small - high], axis=0).astype(BF16)
    cond_grad = cond_grad.T.astype(BF16).reshape(experts, -1, LANES)
    dense = cond_grad.shape[1]
    sums = jnp.concatenate([cond_grad, jnp.broadcast_to(small[None], (experts,) + small.shape)], axis=1)

    grad_layer = matmul(delta, cond_full, 1, 1)
    scaled_front, mean_front = call(
        front_kernel,
        (1,),
        [whole(*half_block), whole(slot_rows, tok_rows), whole(tok_rows, width), whole(1, width)],
        [whole(tok_rows, WIDE * half), whole(tok_rows, 1)],
        [shaped((tok_rows, WIDE * half), F32), shaped((tok_rows, 1), F32)],
        [],
        1_000_000_000,
        6_000_000,
    )(front, gate, tokens, gain_row)
    input_grad = call(
        finish_kernel,
        (1,),
        [
            whole(*half_block),
            whole(tok_rows, WIDE * half),
            whole(tok_rows, 1),
            whole(slot_rows, tok_rows),
            whole(tok_rows, width),
            whole(tok_rows, width),
            whole(tok_rows, 1),
            whole(1, width),
        ],
        whole(tok_rows, width),
        shaped((tok_rows, width), BF16),
        [pltpu.VMEM((tok_rows, WIDE * half), F32)],
        1_000_000_000,
        8_000_000,
    )(back, scaled_front, mean_front, gate, grad_layer, tokens, inverse, gain_row)
    sums = exchange(sums)
    cond_grad, entry_grad, exit_grad, gain_grad, loss_sum = call(
        totals_kernel,
        (1,),
        [whole(*sums.shape)],
        [
            whole(*head_cond.shape),
            whole(*head_in.shape),
            whole(*head_out.shape),
            whole(1, HW),
            whole(1, LANES),
        ],
        [
            shaped(head_cond.shape, F32),
            shaped(head_in.shape, F32),
            shaped(head_out.shape, F32),
            shaped((1, HW), F32),
            shaped((1, LANES), F32),
        ],
        [pltpu.VMEM((dense, LANES), F32), pltpu.VMEM((experts * small_rows, LANES), F32)],
        1_000_000,
        1_000_000,
    )(sums)

    mean_loss = loss_sum[0, 0] / (tok_rows * lax.axis_size(EVERY) * NOISE)
    return (input_grad, cond_grad, entry_grad, exit_grad, gain_grad[0], mean_loss)


def solution(mesh):
    shape = (mesh.shape["dp"] // CORES, CORES, mesh.shape["expert"] // RING, RING)
    fine = Mesh(mesh.devices.reshape(shape), EVERY)
    return jax.shard_map(
        on_device,
        mesh=fine,
        in_specs=(
            P(EVERY, None),
            P(),
            P(EVERY, None),
            P(EVERY, None),
            P(EXPERT, None, None),
            P(EXPERT, None, None),
            P(EVERY, None),
            P(),
            P(),
            P(),
            P(None, EVERY),
            P(None, None, EVERY),
            P(None, EVERY),
        ),
        out_specs=(P(EVERY, None), P(EVERY, None), P(), P(), P(), P()),
        check_vma=False,
    )
```

```python
import math

import jax
import jax.numpy as jnp
from jax import lax
from jax.experimental import pallas as pl
from jax.experimental.pallas import tpu as pltpu
from jax.sharding import Mesh, PartitionSpec as P

HW = 768
TOPK = 4
NOISE = 4
TSTEPS = 1000


NORM_EPS = 1e-06
ROOT_COEF = math.sqrt(2.0 / math.pi)
HIGH = lax.Precision.HIGHEST
DP = ("x", "core")
EXPERT = ("y", "z")
EVERY = DP + EXPERT
CORES = 2
RING = 8
F32 = jnp.float32
BF16 = jnp.bfloat16

MAIN = 16
REST = 8
WIDE = 4
LESS_PART = 256
MORE_PART = 512
HALF_PART = 384
TAIL = 40
NARROW = 3
NARROW_PART = 256
LANES = 128
ENTRY_ROW = 0
EXIT_ROW = 96
GAIN_ROW = 192
LOSS_ROW = 198


def gelu_tanh(values):
    inner = ROOT_COEF * (values + 0.044715 * values * values * values)
    return 0.5 * values * (1.0 + jnp.tanh(inner))


def gelu_slope(values):
    inner = ROOT_COEF * (values + 0.044715 * values * values * values)
    tangent = jnp.tanh(inner)
    return 0.5 * (1.0 + tangent) + 0.5 * values * (1.0 - tangent * tangent) * ROOT_COEF * (
        1.0 + 3.0 * 0.044715 * values * values
    )


def signal_level(step_ids):
    fraction = (step_ids.astype(jnp.float32) / TSTEPS + 0.008) / 1.008
    cosine = jnp.cos(fraction * (math.pi / 2.0))
    return cosine * cosine


def time_embed(step_ids):
    half_width = HW // 2
    frequency = jnp.exp(-math.log(10000.0) * jnp.arange(half_width, dtype=jnp.float32) / half_width)
    angles = step_ids.astype(jnp.float32)[:, None] * frequency[None, :]
    return jnp.concatenate([jnp.cos(angles), jnp.sin(angles)], axis=1)


def matmul(left, right, left_dim=1, right_dim=0, precision=None):
    return lax.dot_general(
        left, right, (((left_dim,), (right_dim,)), ((), ())),
        precision=precision, preferred_element_type=F32,
    )


def iota(shape, axis):
    return lax.broadcasted_iota(jnp.int32, shape, axis)


def of_part(rows, part):
    return ((iota((rows, 1), 0) & 7) >> 1) == part


def rest_rows(peers, part):
    row, col = iota((peers * 2, peers * REST), 0), iota((peers * 2, peers * REST), 1)
    return jnp.where(col == (row >> 1) * REST + part * 2 + (row & 1), 1.0, 0.0).astype(BF16)


def rest_spread(peers, part):
    row, col = iota((peers * REST, peers * 2), 0), iota((peers * REST, peers * 2), 1)
    return jnp.where(row == (col >> 1) * REST + part * 2 + (col & 1), 1.0, 0.0).astype(BF16)


def bring(sources, targets, sems):
    copies = [pltpu.make_async_copy(*ends, sems.at[i]) for i, ends in enumerate(zip(sources, targets))]
    for copy in copies:
        copy.start()
    return copies


def flat(block):
    return block.reshape(block.shape[0] * block.shape[1], block.shape[2])


def main_of(block, part):
    return flat(block[:, MAIN * part : MAIN * (part + 1), :])


def rest_of(block, parts):
    return flat(block[:, MAIN * parts : MAIN * parts + REST, :].astype(F32)).astype(BF16)


def dispatch_kernel(
    tokens_in, gain_in, chosen_in, gates_in, cond_in, send_ref, later_ref, gate_ref, inverse_ref,
    normed_ref, tokens_ref, gain_ref, chosen_ref, gates_ref, cond_ref, own_ref, sems,
):
    step = pl.program_id(0)
    tok_rows = tokens_ref.shape[0]
    experts = gate_ref.shape[0] // (MAIN + REST)
    group = send_ref.shape[0]
    main_rows = experts * MAIN

    @pl.when(step == 0)
    def _():
        sources = (tokens_in, gain_in, chosen_in, gates_in, cond_in)
        for copy in bring(sources, (tokens_ref, gain_ref, chosen_ref, gates_ref, cond_ref), sems):
            copy.wait()
        own_ref[...] = jnp.zeros_like(own_ref)
        cond = cond_ref[...].astype(F32)
        cond_rows = cond.shape[0]
        for piece in range(NARROW):
            columns = slice(piece * NARROW_PART, (piece + 1) * NARROW_PART)
            own_ref[piece * cond_rows : (piece + 1) * cond_rows, :] = cond[:, columns]
        inputs = tokens_ref[...].astype(F32)
        inverse = lax.rsqrt(jnp.mean(inputs * inputs, axis=1, keepdims=True) + NORM_EPS)
        inverse_ref[...] = inverse
        normed_ref[...] = (inputs * inverse * gain_ref[...]).astype(BF16)
        ids = iota((experts, tok_rows), 0)
        named = jnp.zeros((experts, tok_rows), F32)
        gate_of = jnp.zeros((experts, tok_rows), F32)
        for choice in range(TOPK):
            hit = chosen_ref[choice : choice + 1, :] == ids
            named = named + jnp.where(hit, 1.0, 0.0)
            gate_of = gate_of + jnp.where(hit, gates_ref[choice : choice + 1, :], 0.0)
        earlier = jnp.where(iota((tok_rows, tok_rows), 0) < iota((tok_rows, tok_rows), 1), 1.0, 0.0)
        named = named.astype(BF16)
        before = matmul(named, earlier.astype(BF16)).astype(BF16)

        def slots(first, rows, shift, slot):
            spread = jnp.where((iota((rows, experts), 0) >> shift) == iota((rows, experts), 1), 1.0, 0.0)
            spread_bf = spread.astype(BF16)
            held = (matmul(spread_bf, named) > 0.5) & (matmul(spread_bf, before) == slot.astype(F32))
            gates = matmul(spread, gate_of, precision=HIGH)
            gate_ref[first : first + rows, :] = jnp.where(held, gates, 0.0)

        slots(0, main_rows, 4, iota((main_rows, tok_rows), 0) & 15)
        rows = experts * REST
        slots(main_rows, rows, 3, 16 + (iota((rows, tok_rows), 0) & 1))

    main_at = pl.multiple_of(step * (group * MAIN), group * MAIN)
    rest_at = pl.multiple_of(main_rows + step * (group * REST), group * REST)
    pick = jnp.where(gate_ref[pl.ds(main_at, group * MAIN), :] != 0.0, 1.0, 0.0).astype(BF16)
    rest = jnp.where(gate_ref[pl.ds(rest_at, group * REST), :] != 0.0, 1.0, 0.0)
    first = 0
    for out_ref in (send_ref, later_ref):
        width = out_ref.shape[2]
        total = jnp.zeros((group * REST, width), F32)
        for part in range(WIDE):
            piece = normed_ref[:, first : first + width]
            first = first + width
            main = matmul(pick, piece).astype(BF16)
            out_ref[:, MAIN * part : MAIN * (part + 1), :] = main.reshape(group, MAIN, width)
            total = total + matmul(jnp.where(of_part(group * REST, part), rest, 0.0).astype(BF16), piece)
        tail = total.reshape(group, REST, width)
        if out_ref is send_ref:
            own = jnp.broadcast_to(own_ref[...][None], (group,) + own_ref.shape)
            tail = jnp.concatenate([tail, own], axis=1)
        out_ref[:, MAIN * WIDE :, :] = tail.astype(BF16)


def gather_rows(rows_ref, held_ref, part, column):
    peers = rows_ref.shape[0]
    main_rows = peers * MAIN
    main = rows_ref[:, pl.ds(pl.multiple_of(part * MAIN, MAIN), MAIN), :]
    columns = slice(column, column + rows_ref.shape[2])
    held_ref[:main_rows, columns] = flat(main)
    held_ref[main_rows:, columns] = matmul(rest_rows(peers, part), rest_of(rows_ref, WIDE)).astype(BF16)


def first_kernel(rows_ref, up_ref, pre_ref, held_ref):
    step = pl.program_id(0)
    gather_rows(rows_ref, held_ref, 2 * step, 0)
    gather_rows(rows_ref, held_ref, 2 * step + 1, rows_ref.shape[2])
    product = matmul(held_ref[...], up_ref[...])

    @pl.when(step == 0)
    def _():
        pre_ref[...] = product

    @pl.when(step > 0)
    def _():
        pre_ref[...] += product


def forward_kernel(
    rows_ref, up_ref, start_in, mixed_in, pre_ref, hidden_ref, send_ref, held_ref, start_ref, mixed_ref, sems
):
    step = pl.program_id(0)
    start_copy = pltpu.make_async_copy(start_in, start_ref, sems.at[0])
    mixed_copy = pltpu.make_async_copy(mixed_in, mixed_ref, sems.at[1])

    @pl.when(step == 0)
    def _():
        start_copy.start()
        mixed_copy.start()

    peers = rows_ref.shape[0]
    main_rows = peers * MAIN
    gather_rows(rows_ref, held_ref, 2 * step, 0)
    gather_rows(rows_ref, held_ref, 2 * step + 1, rows_ref.shape[2])
    product = matmul(held_ref[...], up_ref[...])

    @pl.when(step == 0)
    def _():
        start_copy.wait()
        pre_ref[...] = start_ref[...] + product

    @pl.when(step == WIDE // 2 - 1)
    def _():
        pre_act = pre_ref[...] + product
        pre_ref[...] = pre_act
        hidden = gelu_tanh(pre_act).astype(BF16)
        hidden_ref[...] = hidden
        mixed_copy.wait()
        added = matmul(hidden, mixed_ref[...]).astype(BF16)
        total = jnp.zeros((peers * REST, NARROW_PART), F32)
        for piece in range(NARROW):
            columns = slice(piece * NARROW_PART, (piece + 1) * NARROW_PART)
            send_ref[:, MAIN * piece : MAIN * (piece + 1), :] = added[:main_rows, columns].reshape(
                peers, MAIN, NARROW_PART
            )
            total = total + matmul(rest_spread(peers, piece), added[main_rows:, columns])
        send_ref[:, MAIN * NARROW :, :] = total.reshape(peers, REST, NARROW_PART).astype(BF16)


def two(values):
    high = values.astype(BF16).astype(F32)
    return jnp.concatenate([high, values - high], axis=values.ndim - 1)


def three(values, axis):
    high = values.astype(BF16)
    left = values - high.astype(F32)
    middle = left.astype(BF16)
    return jnp.concatenate([high, middle, (left - middle.astype(F32)).astype(BF16)], axis=axis)


def of_three(rows):
    third = rows.shape[0] // 3
    return rows[:third] + rows[third : 2 * third] + rows[2 * third :]


def head_kernel(
    added_ref, direct_ref, offset_in, noisy_ref, noise_in, gain_ref, out_in, gate_in,
    delta_ref, send_ref, condition_ref, added_rows_ref, small_ref, offset_ref, noise_ref, out_ref, gate_ref, sems,
):
    copies = bring((gate_in, offset_in, noise_in, out_in), (gate_ref, offset_ref, noise_ref, out_ref), sems)
    copies[0].wait()
    peers = added_ref.shape[0]
    main_rows = peers * MAIN
    gate, gate_rest = gate_ref[:main_rows, :], gate_ref[main_rows:, :]
    rest = rest_of(added_ref, NARROW)
    thirds_rest = three(gate_rest, 1).astype(F32)
    for piece in range(NARROW):
        columns = slice(piece * NARROW_PART, (piece + 1) * NARROW_PART)
        added_rows_ref[:, columns] = main_of(added_ref, piece)
        mine = jnp.where(of_part(peers * REST, piece), thirds_rest, 0.0).astype(BF16)
        condition_ref[:, columns] = direct_ref[:, columns] + of_three(matmul(mine, rest, 0, 0))
    condition_ref[...] += of_three(matmul(three(gate, 1), added_rows_ref[...], 0, 0))
    for copy in copies[1:]:
        copy.wait()
    condition = condition_ref[...]
    gain = gain_ref[...]
    head_out = out_ref[...]
    exit_thirds = jnp.concatenate([head_out, head_out, head_out], axis=0)
    loss = jnp.zeros((1, 1), F32)
    entry_grad = jnp.zeros(head_out.shape, F32)
    exit_grad = jnp.zeros(head_out.shape, F32)
    gain_grad = jnp.zeros_like(gain)
    cond_delta = jnp.zeros_like(condition)
    for draw in range(NOISE):
        state = condition + offset_ref[draw]
        centred = state - jnp.mean(state, axis=1, keepdims=True)
        inv_std = lax.rsqrt(jnp.mean(centred * centred, axis=1, keepdims=True) + NORM_EPS)
        normed = centred * inv_std
        scaled = normed * gain
        sigmoid_val = 1.0 / (1.0 + jnp.exp(-scaled))
        active = (scaled * sigmoid_val).astype(BF16)
        error = matmul(head_out, active, 1, 1) - noise_ref[draw]
        loss = loss + jnp.sum(jnp.sum(error * error, axis=1, keepdims=True), axis=0, keepdims=True)
        grad_pred = three(2.0 / NOISE * error, 0)
        exit_grad = exit_grad + of_three(matmul(grad_pred, active))
        grad_act = matmul(grad_pred, exit_thirds, 0, 0)
        grad_scaled = grad_act * sigmoid_val * (1.0 + scaled * (1.0 - sigmoid_val))
        gain_grad = gain_grad + jnp.sum(grad_scaled * normed, axis=0, keepdims=True)
        grad_normed = grad_scaled * gain
        grad_state = inv_std * (
            grad_normed
            - jnp.mean(grad_normed, axis=1, keepdims=True)
            - normed * jnp.mean(grad_normed * normed, axis=1, keepdims=True)
        )
        noisy = three(noisy_ref[draw], 0)
        high = grad_state.astype(BF16)
        left = (grad_state - high.astype(F32)).astype(BF16)
        entry_grad = entry_grad + of_three(matmul(noisy, high) + matmul(noisy, left))
        cond_delta = cond_delta + grad_state
    delta = cond_delta.astype(BF16)
    delta_ref[...] = delta

    small_ref[...] = jnp.zeros_like(small_ref)
    channels = entry_grad.shape[0]
    for block in range(HW // LANES):
        columns = slice(block * LANES, (block + 1) * LANES)
        at = block * channels
        small_ref[ENTRY_ROW + at : ENTRY_ROW + at + channels, :] = entry_grad[:, columns]
        small_ref[EXIT_ROW + at : EXIT_ROW + at + channels, :] = exit_grad[:, columns]
        small_ref[GAIN_ROW + block : GAIN_ROW + block + 1, :] = gain_grad[:, columns]
    small_ref[LOSS_ROW : LOSS_ROW + 1, :] = jnp.broadcast_to(loss, (1, LANES))
    small = two(small_ref[...].reshape(peers, small_ref.shape[0] // peers, LANES))

    pick = jnp.where(gate != 0.0, 1.0, 0.0).astype(BF16)
    pick_rest = jnp.where(gate_rest != 0.0, 1.0, 0.0)
    slot_gate = jnp.sum(gate, axis=1, keepdims=True)
    total = jnp.zeros((peers * REST, NARROW_PART), F32)
    for piece in range(NARROW):
        columns = delta[:, piece * NARROW_PART : (piece + 1) * NARROW_PART]
        main = (matmul(pick, columns) * slot_gate).astype(BF16)
        send_ref[:, MAIN * piece : MAIN * (piece + 1), :] = main.reshape(peers, MAIN, NARROW_PART)
        mine = jnp.where(of_part(peers * REST, piece), pick_rest, 0.0).astype(BF16)
        total = total + matmul(mine, columns)
    total = total * jnp.sum(gate_rest, axis=1, keepdims=True)
    tail = jnp.concatenate([total.reshape(peers, REST, NARROW_PART), small], axis=1)
    send_ref[:, MAIN * NARROW :, :] = tail.astype(BF16)


def send_back(held_ref, up_ref, send_ref, rest_ref):
    step = pl.program_id(0)
    peers = send_ref.shape[0]
    main_rows = peers * MAIN
    back = matmul(held_ref[...], up_ref[...], 1, 1).astype(BF16)

    @pl.when(step == 0)
    def _():
        rest_ref[...] = jnp.zeros_like(rest_ref)

    width = send_ref.shape[2]
    for side in range(2):
        part = 2 * step + side
        columns = slice(side * width, (side + 1) * width)
        send_ref[:, pl.ds(pl.multiple_of(part * MAIN, MAIN), MAIN), :] = back[:main_rows, columns].reshape(
            peers, MAIN, width
        )
        rest_ref[...] += matmul(rest_spread(peers, part), back[main_rows:, columns])

    @pl.when(step == WIDE // 2 - 1)
    def _():
        send_ref[:, MAIN * WIDE :, :] = rest_ref[...].reshape(peers, REST, width).astype(BF16)


def backward_kernel(
    grads_ref, mixed_in, slope_ref, up_ref, slot_ref, held_ref, small_ref, send_ref, rest_ref, mixed_ref, sem
):
    peers = grads_ref.shape[0]
    main_rows = peers * MAIN

    @pl.when(pl.program_id(0) == 0)
    def _():
        mixed_copy = pltpu.make_async_copy(mixed_in, mixed_ref, sem)
        mixed_copy.start()
        tail = grads_ref[:, MAIN * NARROW :, :].astype(F32)
        rest = flat(tail[:, :REST, :]).astype(BF16)
        for piece in range(NARROW):
            columns = slice(piece * NARROW_PART, (piece + 1) * NARROW_PART)
            slot_ref[:main_rows, columns] = main_of(grads_ref, piece)
            slot_ref[main_rows:, columns] = matmul(rest_rows(peers, piece), rest).astype(BF16)
        mixed_copy.wait()
        grad_hidden = matmul(slot_ref[...], mixed_ref[...], 1, 1)
        held_ref[...] = (grad_hidden * slope_ref[...]).astype(BF16)
        small = jnp.sum(tail[:, REST:, :], axis=0)
        small_ref[...] = small[:, :LANES] + small[:, LANES:]

    send_back(held_ref, up_ref, send_ref, rest_ref)


def second_kernel(held_ref, up_ref, send_ref, rest_ref):
    send_back(held_ref, up_ref, send_ref, rest_ref)


def cond_grad_kernel(slot_ref, hidden_ref, delta_ref, down_ref, tokens_ref, grad_ref, left_ref, right_ref):
    features = down_ref.shape[0]

    @pl.when(pl.program_id(0) == 0)
    def _():
        left_ref[:, :features] = matmul(slot_ref[...], hidden_ref[...], 0, 0).astype(BF16)
        left_ref[:, features:] = delta_ref[...].astype(F32).T.astype(BF16)

    right_ref[:features, :] = down_ref[...]
    right_ref[features:, :] = tokens_ref[...]
    total = matmul(left_ref[...], right_ref[...])
    width = grad_ref.shape[2]
    for side in range(grad_ref.shape[0]):
        grad_ref[side] = total[:, side * width : (side + 1) * width]


def grad_part(block_ref, gate_ref, tokens_ref, gain_ref, scaled_ref, first, mean):
    peers = block_ref.shape[0]
    main_rows = peers * MAIN
    pick = jnp.where(gate_ref[:main_rows, :] != 0.0, 1.0, 0.0).astype(BF16)
    pick_rest = jnp.where(gate_ref[main_rows:, :] != 0.0, 1.0, 0.0)
    rest = rest_of(block_ref, WIDE)
    width = block_ref.shape[2]
    for part in range(WIDE):
        here = slice(part * width, (part + 1) * width)
        columns = slice(first + part * width, first + (part + 1) * width)
        mine = jnp.where(of_part(peers * REST, part), pick_rest, 0.0).astype(BF16)
        total = matmul(pick, main_of(block_ref, part), 0, 0) + matmul(mine, rest, 0, 0)
        scaled = total * gain_ref[:, columns]
        scaled_ref[:, here] = scaled
        mean = mean + jnp.sum(tokens_ref[:, columns].astype(F32) * scaled, axis=1, keepdims=True)
    return mean


def front_kernel(block_ref, gate_ref, tokens_ref, gain_ref, scaled_ref, mean_ref):
    mean_ref[...] = grad_part(block_ref, gate_ref, tokens_ref, gain_ref, scaled_ref, 0, jnp.zeros_like(mean_ref))


def finish_kernel(
    block_ref, front_ref, mean_ref, gate_ref, layer_ref, tokens_ref, inverse_ref, gain_ref, grad_ref, scaled_ref
):
    half = front_ref.shape[1]
    mean = grad_part(block_ref, gate_ref, tokens_ref, gain_ref, scaled_ref, half, mean_ref[...])
    mean = mean / tokens_ref.shape[1]
    inverse = inverse_ref[...]
    cubed = inverse * inverse * inverse * mean
    first = 0
    for part_ref in (front_ref, scaled_ref):
        columns = slice(first, first + part_ref.shape[1])
        first = first + part_ref.shape[1]
        direct = inverse * part_ref[...] - tokens_ref[:, columns].astype(F32) * cubed
        grad_ref[:, columns] = (layer_ref[:, columns] + direct).astype(BF16)


def totals_kernel(sums_ref, cond_ref, entry_ref, exit_ref, gain_ref, loss_ref, total_ref, small_ref):
    dense = total_ref.shape[0]
    peers = sums_ref.shape[0]
    total_ref[...] = jnp.sum(sums_ref[:, :dense, :].astype(F32), axis=0)
    blocks = cond_ref.shape[1] // LANES
    for block in range(blocks):
        cond_ref[:, block * LANES : (block + 1) * LANES] = total_ref[pl.ds(block, dense // blocks, stride=blocks), :]
    small = sums_ref[:, dense:, :].astype(F32)
    small_ref[...] = flat(small[:, :8, :] + small[:, 8:, :])
    channels = entry_ref.shape[0]
    for block in range(blocks):
        columns = slice(block * LANES, (block + 1) * LANES)
        at = block * channels
        entry_ref[:, columns] = small_ref[ENTRY_ROW + at : ENTRY_ROW + at + channels, :]
        exit_ref[:, columns] = small_ref[EXIT_ROW + at : EXIT_ROW + at + channels, :]
        gain_ref[:, columns] = small_ref[GAIN_ROW + block : GAIN_ROW + block + 1, :]
    loss_ref[...] = small_ref[LOSS_ROW : LOSS_ROW + 1, :]


def whole(*shape):
    return pl.BlockSpec(shape, lambda *step: (0,) * len(shape))


def once(*shape):
    return pl.BlockSpec(shape, lambda *step: (0,) * len(shape), pipeline_mode=pl.Buffered(1))


def stored(shape, dtype):
    return pltpu.HBM(shape, dtype)


def shaped(shape, dtype):
    return jax.ShapeDtypeStruct(shape, dtype)


def call(kernel, grid, in_specs, out_specs, out_shape, scratch, flops, moved):
    return pl.pallas_call(
        kernel,
        grid=grid,
        in_specs=in_specs,
        out_specs=out_specs,
        out_shape=out_shape,
        scratch_shapes=scratch,
        compiler_params=pltpu.CompilerParams(vmem_limit_bytes=48 << 20),
        cost_estimate=pl.CostEstimate(flops=flops, bytes_accessed=moved, transcendentals=0),
    )


def exchange(block):
    return lax.all_to_all(block, EXPERT, split_axis=0, concat_axis=0, tiled=True)


def on_device(
    tokens,
    norm_gain,
    experts_chosen,
    gate_weights,
    expert_up,
    expert_down,
    head_cond,
    head_in,
    head_gain,
    head_out,
    latents,
    noise_draws,
    timesteps,
):
    tok_rows, width = tokens.shape
    experts = lax.axis_size(EXPERT)
    features = expert_up.shape[2]
    rows = experts * (MAIN + 2)
    slot_rows = experts * (MAIN + REST)
    less, more = LESS_PART, MORE_PART
    block_rows = WIDE * MAIN + REST
    less_block, more_block = (experts, block_rows, less), (experts, block_rows, more)
    cond_rows = head_cond.shape[0]
    joined = less_block[:1] + (block_rows + TAIL, less)
    half = HALF_PART
    half_block = (experts, block_rows, half)
    narrow_block = (experts, NARROW * MAIN + REST, NARROW_PART)
    grads_block = (experts, NARROW * MAIN + REST + 8, NARROW_PART)
    small_rows = 8
    steps = WIDE // 2
    group = 8
    gain_row = norm_gain.reshape(1, width)
    far = pl.BlockSpec(memory_space=pltpu.HBM)
    weight_up = expert_up[0]
    weight_down = expert_down[0]
    expert_flops = rows * features * width

    send, send_later, gate, inverse = call(
        dispatch_kernel,
        (experts // group,),
        [far, far, far, far, far],
        [
            pl.BlockSpec((group,) + joined[1:], lambda step: (step, 0, 0)),
            pl.BlockSpec((group,) + more_block[1:], lambda step: (step, 0, 0)),
            whole(slot_rows, tok_rows),
            whole(tok_rows, 1),
        ],
        [
            stored(joined, BF16),
            stored(more_block, BF16),
            stored((slot_rows, tok_rows), F32),
            stored((tok_rows, 1), F32),
        ],
        [
            pltpu.VMEM((tok_rows, width), BF16),
            pltpu.VMEM((tok_rows, width), BF16),
            pltpu.VMEM((1, width), F32),
            pltpu.VMEM((TOPK, tok_rows), jnp.int32),
            pltpu.VMEM((TOPK, tok_rows), F32),
            pltpu.VMEM(head_cond.shape, BF16),
            pltpu.VMEM((TAIL, less), F32),
            pltpu.SemaphoreType.DMA((5,)),
        ],
        800_000_000,
        5_000_000,
    )(tokens, gain_row, experts_chosen.T, gate_weights.T, head_cond)

    def of_draws():
        levels = signal_level(timesteps)[:, None, :]
        noisy = jnp.sqrt(levels) * latents[None] + jnp.sqrt(1.0 - levels) * noise_draws
        entered = lax.dot_general(noisy, head_in.astype(F32), (((1,), (0,)), ((), ())), precision=HIGH)
        return entered + time_embed(timesteps.reshape(-1)).reshape(NOISE, tok_rows, HW), noisy

    core = lax.axis_index("core")
    shapes = ((NOISE, tok_rows, HW), noise_draws.shape)
    early = lax.cond(core == 0, of_draws, lambda: tuple(jnp.zeros(shape, F32) for shape in shapes))

    send, early = lax.optimization_barrier((send, early))
    arrived = exchange(send)
    arrived_later = exchange(send_later)
    cond_part = arrived[:, block_rows : block_rows + NARROW * cond_rows, :]
    cond_part = cond_part.reshape(experts, NARROW, cond_rows, NARROW_PART).transpose(0, 2, 1, 3).reshape(-1, HW)
    cond_full = lax.all_gather(cond_part, DP, axis=0, tiled=True)

    down_cond = matmul(weight_down, cond_full).astype(BF16)
    direct = matmul(tokens, cond_full)

    pre_act = call(
        first_kernel,
        (steps,),
        [once(*joined), pl.BlockSpec((2 * less, features), lambda step: (step, 0))],
        whole(rows, features),
        stored((rows, features), F32),
        [pltpu.VMEM((rows, 2 * less), BF16)],
        expert_flops,
        6_000_000,
    )(arrived, weight_up)
    pre_act, hidden, send = call(
        forward_kernel,
        (steps,),
        [
            once(*more_block),
            pl.BlockSpec((2 * more, features), lambda step: (step + 1, 0)),
            far,
            far,
        ],
        [whole(rows, features), whole(rows, features), whole(*narrow_block)],
        [stored((rows, features), F32), stored((rows, features), BF16), stored(narrow_block, BF16)],
        [
            pltpu.VMEM((rows, 2 * more), BF16),
            pltpu.VMEM((rows, features), F32),
            pltpu.VMEM((features, HW), BF16),
            pltpu.SemaphoreType.DMA((2,)),
        ],
        2 * expert_flops,
        10_000_000,
    )(arrived_later, weight_up, pre_act, down_cond)
    added = exchange(send)
    offset, noisy = lax.cond(core == 1, of_draws, lambda: early)
    slope = gelu_slope(pre_act)

    delta, send = call(
        head_kernel,
        (1,),
        [
            whole(*narrow_block),
            whole(tok_rows, HW),
            far,
            whole(*noisy.shape),
            far,
            whole(1, HW),
            far,
            far,
        ],
        [whole(tok_rows, HW), whole(*grads_block)],
        [stored((tok_rows, HW), BF16), stored(grads_block, BF16)],
        [
            pltpu.VMEM((tok_rows, HW), F32),
            pltpu.VMEM((experts * MAIN, HW), BF16),
            pltpu.VMEM((experts * small_rows, LANES), F32),
            pltpu.VMEM((NOISE, tok_rows, HW), F32),
            pltpu.VMEM(noise_draws.shape, F32),
            pltpu.VMEM(head_out.shape, BF16),
            pltpu.VMEM((slot_rows, tok_rows), F32),
            pltpu.SemaphoreType.DMA((4,)),
        ],
        1_500_000_000,
        5_000_000,
    )(added, direct, offset, noisy, noise_draws, head_gain.reshape(1, HW), head_out, gate)
    arrived = exchange(send)

    slot_grads, held, small, send = call(
        backward_kernel,
        (steps,),
        [
            once(*grads_block),
            far,
            once(rows, features),
            pl.BlockSpec((2 * half, features), lambda step: (step, 0)),
        ],
        [whole(rows, HW), whole(rows, features), whole(small_rows, LANES), whole(*half_block)],
        [
            stored((rows, HW), BF16),
            stored((rows, features), BF16),
            stored((small_rows, LANES), F32),
            stored(half_block, BF16),
        ],
        [
            pltpu.VMEM((experts * REST, half), F32),
            pltpu.VMEM((features, HW), BF16),
            pltpu.SemaphoreType.DMA,
        ],
        2 * expert_flops,
        10_000_000,
    )(arrived, down_cond, slope, weight_up)
    slot_grads, held, small, send = lax.optimization_barrier((slot_grads, held, small, send))
    front = exchange(send)
    send = call(
        second_kernel,
        (steps,),
        [once(rows, features), pl.BlockSpec((2 * half, features), lambda step: (step + steps, 0))],
        whole(*half_block),
        stored(half_block, BF16),
        [pltpu.VMEM((experts * REST, half), F32)],
        0,
        0,
    )(held, weight_up)

    back = exchange(send)

    chunks = lax.axis_size(DP)
    chunk = width // chunks
    cond_grad = call(
        cond_grad_kernel,
        (chunks // 2,),
        [
            once(rows, HW),
            once(rows, features),
            once(tok_rows, HW),
            pl.BlockSpec((features, 2 * chunk), lambda step: (0, step)),
            pl.BlockSpec((tok_rows, 2 * chunk), lambda step: (0, step)),
        ],
        pl.BlockSpec((2, HW, chunk), lambda step: (step, 0, 0)),
        stored((chunks, HW, chunk), F32),
        [pltpu.VMEM((HW, features + tok_rows), BF16), pltpu.VMEM((features + tok_rows, 2 * chunk), BF16)],
        0,
        0,
    )(slot_grads, hidden, delta, weight_down, tokens)
    cond_grad = lax.psum_scatter(cond_grad, DP, scatter_dimension=0, tiled=True)[0]
    small, front = lax.optimization_barrier((small, front))
    small = lax.all_gather(small, DP, axis=0, tiled=True)
    small = jnp.sum(small.reshape(-1, small_rows, LANES), axis=0)
    high = lax.reduce_precision(small, 8, 7)
    small = jnp.concatenate([high, small - high], axis=0).astype(BF16)
    cond_grad = cond_grad.T.astype(BF16).reshape(experts, -1, LANES)
    dense = cond_grad.shape[1]
    sums = jnp.concatenate([cond_grad, jnp.broadcast_to(small[None], (experts,) + small.shape)], axis=1)

    grad_layer = matmul(delta, cond_full, 1, 1)
    scaled_front, mean_front = call(
        front_kernel,
        (1,),
        [whole(*half_block), whole(slot_rows, tok_rows), whole(tok_rows, width), whole(1, width)],
        [whole(tok_rows, WIDE * half), whole(tok_rows, 1)],
        [shaped((tok_rows, WIDE * half), F32), shaped((tok_rows, 1), F32)],
        [],
        1_000_000_000,
        6_000_000,
    )(front, gate, tokens, gain_row)
    input_grad = call(
        finish_kernel,
        (1,),
        [
            whole(*half_block),
            whole(tok_rows, WIDE * half),
            whole(tok_rows, 1),
            whole(slot_rows, tok_rows),
            whole(tok_rows, width),
            whole(tok_rows, width),
            whole(tok_rows, 1),
            whole(1, width),
        ],
        whole(tok_rows, width),
        shaped((tok_rows, width), BF16),
        [pltpu.VMEM((tok_rows, WIDE * half), F32)],
        1_000_000_000,
        8_000_000,
    )(back, scaled_front, mean_front, gate, grad_layer, tokens, inverse, gain_row)
    sums = exchange(sums)
    cond_grad, entry_grad, exit_grad, gain_grad, loss_sum = call(
        totals_kernel,
        (1,),
        [whole(*sums.shape)],
        [
            whole(*head_cond.shape),
            whole(*head_in.shape),
            whole(*head_out.shape),
            whole(1, HW),
            whole(1, LANES),
        ],
        [
            shaped(head_cond.shape, F32),
            shaped(head_in.shape, F32),
            shaped(head_out.shape, F32),
            shaped((1, HW), F32),
            shaped((1, LANES), F32),
        ],
        [pltpu.VMEM((dense, LANES), F32), pltpu.VMEM((experts * small_rows, LANES), F32)],
        1_000_000,
        1_000_000,
    )(sums)

    mean_loss = loss_sum[0, 0] / (tok_rows * lax.axis_size(EVERY) * NOISE)
    return (input_grad, cond_grad, entry_grad, exit_grad, gain_grad[0], mean_loss)


def solution(mesh):
    shape = (mesh.shape["dp"] // CORES, CORES, mesh.shape["expert"] // RING, RING)
    fine = Mesh(mesh.devices.reshape(shape), EVERY)
    return jax.shard_map(
        on_device,
        mesh=fine,
        in_specs=(
            P(EVERY, None),
            P(),
            P(EVERY, None),
            P(EVERY, None),
            P(EXPERT, None, None),
            P(EXPERT, None, None),
            P(EVERY, None),
            P(),
            P(),
            P(),
            P(None, EVERY),
            P(None, None, EVERY),
            P(None, EVERY),
        ),
        out_specs=(P(EVERY, None), P(EVERY, None), P(), P(), P(), P()),
        check_vma=False,
    )
```

```python
import math

import jax
import jax.numpy as jnp
from jax import lax
from jax.experimental import pallas as pl
from jax.experimental.pallas import tpu as pltpu
from jax.sharding import Mesh, PartitionSpec as P

HW = 768
TOPK = 4
NOISE = 4
TSTEPS = 1000


NORM_EPS = 1e-06
ROOT_COEF = math.sqrt(2.0 / math.pi)
HIGH = lax.Precision.HIGHEST
DP = ("x", "core")
EXPERT = ("y", "z")
EVERY = DP + EXPERT
CORES = 2
RING = 8
F32 = jnp.float32
BF16 = jnp.bfloat16

MAIN = 16
REST = 8
WIDE = 4
LESS_PART = 256
MORE_PART = 512
HALF_PART = 384
TAIL = 40
NARROW = 3
NARROW_PART = 256
LANES = 128
ENTRY_ROW = 0
EXIT_ROW = 96
GAIN_ROW = 192
LOSS_ROW = 198


def gelu_tanh(values):
    inner = ROOT_COEF * (values + 0.044715 * values * values * values)
    return 0.5 * values * (1.0 + jnp.tanh(inner))


def gelu_slope(values):
    inner = ROOT_COEF * (values + 0.044715 * values * values * values)
    tangent = jnp.tanh(inner)
    return 0.5 * (1.0 + tangent) + 0.5 * values * (1.0 - tangent * tangent) * ROOT_COEF * (
        1.0 + 3.0 * 0.044715 * values * values
    )


def signal_level(step_ids):
    fraction = (step_ids.astype(jnp.float32) / TSTEPS + 0.008) / 1.008
    cosine = jnp.cos(fraction * (math.pi / 2.0))
    return cosine * cosine


def time_embed(step_ids):
    half_width = HW // 2
    frequency = jnp.exp(-math.log(10000.0) * jnp.arange(half_width, dtype=jnp.float32) / half_width)
    angles = step_ids.astype(jnp.float32)[:, None] * frequency[None, :]
    return jnp.concatenate([jnp.cos(angles), jnp.sin(angles)], axis=1)


def matmul(left, right, left_dim=1, right_dim=0, precision=None):
    return lax.dot_general(
        left, right, (((left_dim,), (right_dim,)), ((), ())),
        precision=precision, preferred_element_type=F32,
    )


def iota(shape, axis):
    return lax.broadcasted_iota(jnp.int32, shape, axis)


def of_part(rows, part):
    return ((iota((rows, 1), 0) & 7) >> 1) == part


def rest_rows(peers, part):
    row, col = iota((peers * 2, peers * REST), 0), iota((peers * 2, peers * REST), 1)
    return jnp.where(col == (row >> 1) * REST + part * 2 + (row & 1), 1.0, 0.0).astype(BF16)


def rest_spread(peers, part):
    row, col = iota((peers * REST, peers * 2), 0), iota((peers * REST, peers * 2), 1)
    return jnp.where(row == (col >> 1) * REST + part * 2 + (col & 1), 1.0, 0.0).astype(BF16)


def bring(sources, targets, sems):
    copies = [pltpu.make_async_copy(*ends, sems.at[i]) for i, ends in enumerate(zip(sources, targets))]
    for copy in copies:
        copy.start()
    return copies


def flat(block):
    return block.reshape(block.shape[0] * block.shape[1], block.shape[2])


def main_of(block, part):
    return flat(block[:, MAIN * part : MAIN * (part + 1), :])


def rest_of(block, parts):
    return flat(block[:, MAIN * parts : MAIN * parts + REST, :].astype(F32)).astype(BF16)


def dispatch_kernel(
    tokens_in, gain_in, chosen_in, gates_in, cond_in, send_ref, later_ref, gate_ref, inverse_ref,
    normed_ref, tokens_ref, gain_ref, chosen_ref, gates_ref, cond_ref, own_ref, sems,
):
    step = pl.program_id(0)
    tok_rows = tokens_ref.shape[0]
    experts = gate_ref.shape[0] // (MAIN + REST)
    group = send_ref.shape[0]
    main_rows = experts * MAIN

    @pl.when(step == 0)
    def _():
        sources = (tokens_in, gain_in, chosen_in, gates_in, cond_in)
        for copy in bring(sources, (tokens_ref, gain_ref, chosen_ref, gates_ref, cond_ref), sems):
            copy.wait()
        own_ref[...] = jnp.zeros_like(own_ref)
        cond = cond_ref[...].astype(F32)
        cond_rows = cond.shape[0]
        for piece in range(NARROW):
            columns = slice(piece * NARROW_PART, (piece + 1) * NARROW_PART)
            own_ref[piece * cond_rows : (piece + 1) * cond_rows, :] = cond[:, columns]
        inputs = tokens_ref[...].astype(F32)
        inverse = lax.rsqrt(jnp.mean(inputs * inputs, axis=1, keepdims=True) + NORM_EPS)
        inverse_ref[...] = inverse
        normed_ref[...] = (inputs * inverse * gain_ref[...]).astype(BF16)
        ids = iota((experts, tok_rows), 0)
        named = jnp.zeros((experts, tok_rows), F32)
        gate_of = jnp.zeros((experts, tok_rows), F32)
        for choice in range(TOPK):
            hit = chosen_ref[choice : choice + 1, :] == ids
            named = named + jnp.where(hit, 1.0, 0.0)
            gate_of = gate_of + jnp.where(hit, gates_ref[choice : choice + 1, :], 0.0)
        earlier = jnp.where(iota((tok_rows, tok_rows), 0) < iota((tok_rows, tok_rows), 1), 1.0, 0.0)
        named = named.astype(BF16)
        before = matmul(named, earlier.astype(BF16)).astype(BF16)

        def slots(first, rows, shift, slot):
            spread = jnp.where((iota((rows, experts), 0) >> shift) == iota((rows, experts), 1), 1.0, 0.0)
            spread_bf = spread.astype(BF16)
            held = (matmul(spread_bf, named) > 0.5) & (matmul(spread_bf, before) == slot.astype(F32))
            gates = matmul(spread, gate_of, precision=HIGH)
            gate_ref[first : first + rows, :] = jnp.where(held, gates, 0.0)

        slots(0, main_rows, 4, iota((main_rows, tok_rows), 0) & 15)
        rows = experts * REST
        slots(main_rows, rows, 3, 16 + (iota((rows, tok_rows), 0) & 1))

    main_at = pl.multiple_of(step * (group * MAIN), group * MAIN)
    rest_at = pl.multiple_of(main_rows + step * (group * REST), group * REST)
    pick = jnp.where(gate_ref[pl.ds(main_at, group * MAIN), :] != 0.0, 1.0, 0.0).astype(BF16)
    rest = jnp.where(gate_ref[pl.ds(rest_at, group * REST), :] != 0.0, 1.0, 0.0)
    first = 0
    for out_ref in (send_ref, later_ref):
        width = out_ref.shape[2]
        total = jnp.zeros((group * REST, width), F32)
        for part in range(WIDE):
            piece = normed_ref[:, first : first + width]
            first = first + width
            main = matmul(pick, piece).astype(BF16)
            out_ref[:, MAIN * part : MAIN * (part + 1), :] = main.reshape(group, MAIN, width)
            total = total + matmul(jnp.where(of_part(group * REST, part), rest, 0.0).astype(BF16), piece)
        tail = total.reshape(group, REST, width)
        if out_ref is send_ref:
            own = jnp.broadcast_to(own_ref[...][None], (group,) + own_ref.shape)
            tail = jnp.concatenate([tail, own], axis=1)
        out_ref[:, MAIN * WIDE :, :] = tail.astype(BF16)


def gather_rows(rows_ref, held_ref, part, column):
    peers = rows_ref.shape[0]
    main_rows = peers * MAIN
    main = rows_ref[:, pl.ds(pl.multiple_of(part * MAIN, MAIN), MAIN), :]
    columns = slice(column, column + rows_ref.shape[2])
    held_ref[:main_rows, columns] = flat(main)
    held_ref[main_rows:, columns] = matmul(rest_rows(peers, part), rest_of(rows_ref, WIDE)).astype(BF16)


def first_kernel(rows_ref, up_ref, pre_ref, held_ref):
    step = pl.program_id(0)
    gather_rows(rows_ref, held_ref, 2 * step, 0)
    gather_rows(rows_ref, held_ref, 2 * step + 1, rows_ref.shape[2])
    product = matmul(held_ref[...], up_ref[...])

    @pl.when(step == 0)
    def _():
        pre_ref[...] = product

    @pl.when(step > 0)
    def _():
        pre_ref[...] += product


def forward_kernel(
    rows_ref, up_ref, start_in, mixed_in, pre_ref, hidden_ref, send_ref, held_ref, start_ref, mixed_ref, sems
):
    step = pl.program_id(0)
    start_copy = pltpu.make_async_copy(start_in, start_ref, sems.at[0])
    mixed_copy = pltpu.make_async_copy(mixed_in, mixed_ref, sems.at[1])

    @pl.when(step == 0)
    def _():
        start_copy.start()
        mixed_copy.start()

    peers = rows_ref.shape[0]
    main_rows = peers * MAIN
    gather_rows(rows_ref, held_ref, 2 * step, 0)
    gather_rows(rows_ref, held_ref, 2 * step + 1, rows_ref.shape[2])
    product = matmul(held_ref[...], up_ref[...])

    @pl.when(step == 0)
    def _():
        start_copy.wait()
        pre_ref[...] = start_ref[...] + product

    @pl.when(step == WIDE // 2 - 1)
    def _():
        pre_act = pre_ref[...] + product
        pre_ref[...] = pre_act
        hidden = gelu_tanh(pre_act).astype(BF16)
        hidden_ref[...] = hidden
        mixed_copy.wait()
        added = matmul(hidden, mixed_ref[...]).astype(BF16)
        total = jnp.zeros((peers * REST, NARROW_PART), F32)
        for piece in range(NARROW):
            columns = slice(piece * NARROW_PART, (piece + 1) * NARROW_PART)
            send_ref[:, MAIN * piece : MAIN * (piece + 1), :] = added[:main_rows, columns].reshape(
                peers, MAIN, NARROW_PART
            )
            total = total + matmul(rest_spread(peers, piece), added[main_rows:, columns])
        send_ref[:, MAIN * NARROW :, :] = total.reshape(peers, REST, NARROW_PART).astype(BF16)


def two(values):
    high = values.astype(BF16).astype(F32)
    return jnp.concatenate([high, values - high], axis=values.ndim - 1)


def three(values, axis):
    high = values.astype(BF16)
    left = values - high.astype(F32)
    middle = left.astype(BF16)
    return jnp.concatenate([high, middle, (left - middle.astype(F32)).astype(BF16)], axis=axis)


def of_three(rows):
    third = rows.shape[0] // 3
    return rows[:third] + rows[third : 2 * third] + rows[2 * third :]


def head_kernel(
    added_ref, direct_ref, offset_in, noisy_ref, noise_in, gain_ref, out_in, gate_in,
    delta_ref, send_ref, condition_ref, added_rows_ref, small_ref, offset_ref, noise_ref, out_ref, gate_ref, sems,
):
    copies = bring((gate_in, offset_in, noise_in, out_in), (gate_ref, offset_ref, noise_ref, out_ref), sems)
    copies[0].wait()
    peers = added_ref.shape[0]
    main_rows = peers * MAIN
    gate, gate_rest = gate_ref[:main_rows, :], gate_ref[main_rows:, :]
    rest = rest_of(added_ref, NARROW)
    thirds_rest = three(gate_rest, 1).astype(F32)
    for piece in range(NARROW):
        columns = slice(piece * NARROW_PART, (piece + 1) * NARROW_PART)
        added_rows_ref[:, columns] = main_of(added_ref, piece)
        mine = jnp.where(of_part(peers * REST, piece), thirds_rest, 0.0).astype(BF16)
        condition_ref[:, columns] = direct_ref[:, columns] + of_three(matmul(mine, rest, 0, 0))
    condition_ref[...] += of_three(matmul(three(gate, 1), added_rows_ref[...], 0, 0))
    for copy in copies[1:]:
        copy.wait()
    condition = condition_ref[...]
    gain = gain_ref[...]
    head_out = out_ref[...]
    exit_thirds = jnp.concatenate([head_out, head_out, head_out], axis=0)
    loss = jnp.zeros((1, 1), F32)
    entry_grad = jnp.zeros(head_out.shape, F32)
    exit_grad = jnp.zeros(head_out.shape, F32)
    gain_grad = jnp.zeros_like(gain)
    cond_delta = jnp.zeros_like(condition)
    for draw in range(NOISE):
        state = condition + offset_ref[draw]
        centred = state - jnp.mean(state, axis=1, keepdims=True)
        inv_std = lax.rsqrt(jnp.mean(centred * centred, axis=1, keepdims=True) + NORM_EPS)
        normed = centred * inv_std
        scaled = normed * gain
        sigmoid_val = 1.0 / (1.0 + jnp.exp(-scaled))
        active = (scaled * sigmoid_val).astype(BF16)
        error = matmul(head_out, active, 1, 1) - noise_ref[draw]
        loss = loss + jnp.sum(jnp.sum(error * error, axis=1, keepdims=True), axis=0, keepdims=True)
        grad_pred = three(2.0 / NOISE * error, 0)
        exit_grad = exit_grad + of_three(matmul(grad_pred, active))
        grad_act = matmul(grad_pred, exit_thirds, 0, 0)
        grad_scaled = grad_act * sigmoid_val * (1.0 + scaled * (1.0 - sigmoid_val))
        gain_grad = gain_grad + jnp.sum(grad_scaled * normed, axis=0, keepdims=True)
        grad_normed = grad_scaled * gain
        grad_state = inv_std * (
            grad_normed
            - jnp.mean(grad_normed, axis=1, keepdims=True)
            - normed * jnp.mean(grad_normed * normed, axis=1, keepdims=True)
        )
        noisy = three(noisy_ref[draw], 0)
        high = grad_state.astype(BF16)
        left = (grad_state - high.astype(F32)).astype(BF16)
        entry_grad = entry_grad + of_three(matmul(noisy, high) + matmul(noisy, left))
        cond_delta = cond_delta + grad_state
    delta = cond_delta.astype(BF16)
    delta_ref[...] = delta

    small_ref[...] = jnp.zeros_like(small_ref)
    channels = entry_grad.shape[0]
    for block in range(HW // LANES):
        columns = slice(block * LANES, (block + 1) * LANES)
        at = block * channels
        small_ref[ENTRY_ROW + at : ENTRY_ROW + at + channels, :] = entry_grad[:, columns]
        small_ref[EXIT_ROW + at : EXIT_ROW + at + channels, :] = exit_grad[:, columns]
        small_ref[GAIN_ROW + block : GAIN_ROW + block + 1, :] = gain_grad[:, columns]
    small_ref[LOSS_ROW : LOSS_ROW + 1, :] = jnp.broadcast_to(loss, (1, LANES))
    small = two(small_ref[...].reshape(peers, small_ref.shape[0] // peers, LANES))

    pick = jnp.where(gate != 0.0, 1.0, 0.0).astype(BF16)
    pick_rest = jnp.where(gate_rest != 0.0, 1.0, 0.0)
    slot_gate = jnp.sum(gate, axis=1, keepdims=True)
    total = jnp.zeros((peers * REST, NARROW_PART), F32)
    for piece in range(NARROW):
        columns = delta[:, piece * NARROW_PART : (piece + 1) * NARROW_PART]
        main = (matmul(pick, columns) * slot_gate).astype(BF16)
        send_ref[:, MAIN * piece : MAIN * (piece + 1), :] = main.reshape(peers, MAIN, NARROW_PART)
        mine = jnp.where(of_part(peers * REST, piece), pick_rest, 0.0).astype(BF16)
        total = total + matmul(mine, columns)
    total = total * jnp.sum(gate_rest, axis=1, keepdims=True)
    tail = jnp.concatenate([total.reshape(peers, REST, NARROW_PART), small], axis=1)
    send_ref[:, MAIN * NARROW :, :] = tail.astype(BF16)


def send_back(held_ref, up_ref, send_ref, rest_ref):
    step = pl.program_id(0)
    peers = send_ref.shape[0]
    main_rows = peers * MAIN
    back = matmul(held_ref[...], up_ref[...], 1, 1).astype(BF16)

    @pl.when(step == 0)
    def _():
        rest_ref[...] = jnp.zeros_like(rest_ref)

    width = send_ref.shape[2]
    for side in range(2):
        part = 2 * step + side
        columns = slice(side * width, (side + 1) * width)
        send_ref[:, pl.ds(pl.multiple_of(part * MAIN, MAIN), MAIN), :] = back[:main_rows, columns].reshape(
            peers, MAIN, width
        )
        rest_ref[...] += matmul(rest_spread(peers, part), back[main_rows:, columns])

    @pl.when(step == WIDE // 2 - 1)
    def _():
        send_ref[:, MAIN * WIDE :, :] = rest_ref[...].reshape(peers, REST, width).astype(BF16)


def backward_kernel(
    grads_ref, mixed_in, slope_ref, up_ref, slot_ref, held_ref, small_ref, send_ref, rest_ref, mixed_ref, sem
):
    peers = grads_ref.shape[0]
    main_rows = peers * MAIN

    @pl.when(pl.program_id(0) == 0)
    def _():
        mixed_copy = pltpu.make_async_copy(mixed_in, mixed_ref, sem)
        mixed_copy.start()
        tail = grads_ref[:, MAIN * NARROW :, :].astype(F32)
        rest = flat(tail[:, :REST, :]).astype(BF16)
        for piece in range(NARROW):
            columns = slice(piece * NARROW_PART, (piece + 1) * NARROW_PART)
            slot_ref[:main_rows, columns] = main_of(grads_ref, piece)
            slot_ref[main_rows:, columns] = matmul(rest_rows(peers, piece), rest).astype(BF16)
        mixed_copy.wait()
        grad_hidden = matmul(slot_ref[...], mixed_ref[...], 1, 1)
        held_ref[...] = (grad_hidden * slope_ref[...]).astype(BF16)
        small = jnp.sum(tail[:, REST:, :], axis=0)
        small_ref[...] = small[:, :LANES] + small[:, LANES:]

    send_back(held_ref, up_ref, send_ref, rest_ref)


def second_kernel(held_ref, up_ref, send_ref, rest_ref):
    send_back(held_ref, up_ref, send_ref, rest_ref)


def cond_grad_kernel(hidden_ref, slot_ref, down_ref, tokens_ref, delta_ref, grad_ref, both_ref):
    @pl.when(pl.program_id(0) == 0)
    def _():
        both_ref[...] = matmul(hidden_ref[...], slot_ref[...], 0, 0).astype(BF16)

    total = matmul(down_ref[...], both_ref[...], 0, 0) + matmul(tokens_ref[...], delta_ref[...], 0, 0)
    grad_ref[...] = total.astype(BF16)


def grad_part(block_ref, gate_ref, tokens_ref, gain_ref, scaled_ref, first, mean):
    peers = block_ref.shape[0]
    main_rows = peers * MAIN
    pick = jnp.where(gate_ref[:main_rows, :] != 0.0, 1.0, 0.0).astype(BF16)
    pick_rest = jnp.where(gate_ref[main_rows:, :] != 0.0, 1.0, 0.0)
    rest = rest_of(block_ref, WIDE)
    width = block_ref.shape[2]
    for part in range(WIDE):
        here = slice(part * width, (part + 1) * width)
        columns = slice(first + part * width, first + (part + 1) * width)
        mine = jnp.where(of_part(peers * REST, part), pick_rest, 0.0).astype(BF16)
        total = matmul(pick, main_of(block_ref, part), 0, 0) + matmul(mine, rest, 0, 0)
        scaled = total * gain_ref[:, columns]
        scaled_ref[:, here] = scaled
        mean = mean + jnp.sum(tokens_ref[:, columns].astype(F32) * scaled, axis=1, keepdims=True)
    return mean


def front_kernel(block_ref, gate_ref, tokens_ref, gain_ref, scaled_ref, mean_ref):
    mean_ref[...] = grad_part(block_ref, gate_ref, tokens_ref, gain_ref, scaled_ref, 0, jnp.zeros_like(mean_ref))


def finish_kernel(
    block_ref, front_ref, mean_ref, gate_ref, layer_ref, tokens_ref, inverse_ref, gain_ref, grad_ref, scaled_ref
):
    half = front_ref.shape[1]
    mean = grad_part(block_ref, gate_ref, tokens_ref, gain_ref, scaled_ref, half, mean_ref[...])
    mean = mean / tokens_ref.shape[1]
    inverse = inverse_ref[...]
    cubed = inverse * inverse * inverse * mean
    first = 0
    for part_ref in (front_ref, scaled_ref):
        columns = slice(first, first + part_ref.shape[1])
        first = first + part_ref.shape[1]
        direct = inverse * part_ref[...] - tokens_ref[:, columns].astype(F32) * cubed
        grad_ref[:, columns] = (layer_ref[:, columns] + direct).astype(BF16)


def totals_kernel(sums_ref, cond_ref, entry_ref, exit_ref, gain_ref, loss_ref, total_ref, small_ref):
    dense = total_ref.shape[0]
    peers = sums_ref.shape[0]
    total_ref[...] = jnp.sum(sums_ref[:, :dense, :].astype(F32), axis=0)
    blocks = cond_ref.shape[1] // LANES
    for block in range(blocks):
        cond_ref[:, block * LANES : (block + 1) * LANES] = total_ref[pl.ds(block, dense // blocks, stride=blocks), :]
    for line in range((sums_ref.shape[1] - dense) // 16):
        first = dense + line * 16
        small = sums_ref[:, first : first + 16, :].astype(F32)
        small_ref[line * peers * 8 : (line + 1) * peers * 8, :] = flat(small[:, :8, :] + small[:, 8:, :])
    channels = entry_ref.shape[0]
    for block in range(blocks):
        columns = slice(block * LANES, (block + 1) * LANES)
        at = block * channels
        entry_ref[:, columns] = small_ref[ENTRY_ROW + at : ENTRY_ROW + at + channels, :]
        exit_ref[:, columns] = small_ref[EXIT_ROW + at : EXIT_ROW + at + channels, :]
        gain_ref[:, columns] = small_ref[GAIN_ROW + block : GAIN_ROW + block + 1, :]
    loss_ref[...] = small_ref[LOSS_ROW : LOSS_ROW + 1, :]


def whole(*shape):
    return pl.BlockSpec(shape, lambda *step: (0,) * len(shape))


def once(*shape):
    return pl.BlockSpec(shape, lambda *step: (0,) * len(shape), pipeline_mode=pl.Buffered(1))


def stored(shape, dtype):
    return pltpu.HBM(shape, dtype)


def shaped(shape, dtype):
    return jax.ShapeDtypeStruct(shape, dtype)


def call(kernel, grid, in_specs, out_specs, out_shape, scratch, flops, moved):
    return pl.pallas_call(
        kernel,
        grid=grid,
        in_specs=in_specs,
        out_specs=out_specs,
        out_shape=out_shape,
        scratch_shapes=scratch,
        compiler_params=pltpu.CompilerParams(vmem_limit_bytes=48 << 20),
        cost_estimate=pl.CostEstimate(flops=flops, bytes_accessed=moved, transcendentals=0),
    )


def exchange(block):
    return lax.all_to_all(block, EXPERT, split_axis=0, concat_axis=0, tiled=True)


def on_device(
    tokens,
    norm_gain,
    experts_chosen,
    gate_weights,
    expert_up,
    expert_down,
    head_cond,
    head_in,
    head_gain,
    head_out,
    latents,
    noise_draws,
    timesteps,
):
    tok_rows, width = tokens.shape
    experts = lax.axis_size(EXPERT)
    features = expert_up.shape[2]
    rows = experts * (MAIN + 2)
    slot_rows = experts * (MAIN + REST)
    less, more = LESS_PART, MORE_PART
    block_rows = WIDE * MAIN + REST
    less_block, more_block = (experts, block_rows, less), (experts, block_rows, more)
    cond_rows = head_cond.shape[0]
    joined = less_block[:1] + (block_rows + TAIL, less)
    half = HALF_PART
    half_block = (experts, block_rows, half)
    narrow_block = (experts, NARROW * MAIN + REST, NARROW_PART)
    grads_block = (experts, NARROW * MAIN + REST + 8, NARROW_PART)
    small_rows = 8
    steps = WIDE // 2
    group = 8
    gain_row = norm_gain.reshape(1, width)
    far = pl.BlockSpec(memory_space=pltpu.HBM)
    weight_up = expert_up[0]
    weight_down = expert_down[0]
    expert_flops = rows * features * width

    send, send_later, gate, inverse = call(
        dispatch_kernel,
        (experts // group,),
        [far, far, far, far, far],
        [
            pl.BlockSpec((group,) + joined[1:], lambda step: (step, 0, 0)),
            pl.BlockSpec((group,) + more_block[1:], lambda step: (step, 0, 0)),
            whole(slot_rows, tok_rows),
            whole(tok_rows, 1),
        ],
        [
            stored(joined, BF16),
            stored(more_block, BF16),
            stored((slot_rows, tok_rows), F32),
            stored((tok_rows, 1), F32),
        ],
        [
            pltpu.VMEM((tok_rows, width), BF16),
            pltpu.VMEM((tok_rows, width), BF16),
            pltpu.VMEM((1, width), F32),
            pltpu.VMEM((TOPK, tok_rows), jnp.int32),
            pltpu.VMEM((TOPK, tok_rows), F32),
            pltpu.VMEM(head_cond.shape, BF16),
            pltpu.VMEM((TAIL, less), F32),
            pltpu.SemaphoreType.DMA((5,)),
        ],
        800_000_000,
        5_000_000,
    )(tokens, gain_row, experts_chosen.T, gate_weights.T, head_cond)

    def of_draws():
        levels = signal_level(timesteps)[:, None, :]
        noisy = jnp.sqrt(levels) * latents[None] + jnp.sqrt(1.0 - levels) * noise_draws
        entered = lax.dot_general(noisy, head_in.astype(F32), (((1,), (0,)), ((), ())), precision=HIGH)
        return entered + time_embed(timesteps.reshape(-1)).reshape(NOISE, tok_rows, HW), noisy

    core = lax.axis_index("core")
    shapes = ((NOISE, tok_rows, HW), noise_draws.shape)
    early = lax.cond(core == 0, of_draws, lambda: tuple(jnp.zeros(shape, F32) for shape in shapes))

    send, early = lax.optimization_barrier((send, early))
    arrived = exchange(send)
    arrived_later = exchange(send_later)
    cond_part = arrived[:, block_rows : block_rows + NARROW * cond_rows, :]
    cond_part = cond_part.reshape(experts, NARROW, cond_rows, NARROW_PART).transpose(0, 2, 1, 3).reshape(-1, HW)
    cond_full = lax.all_gather(cond_part, DP, axis=0, tiled=True)

    down_cond = matmul(weight_down, cond_full).astype(BF16)
    direct = matmul(tokens, cond_full)

    pre_act = call(
        first_kernel,
        (steps,),
        [once(*joined), pl.BlockSpec((2 * less, features), lambda step: (step, 0))],
        whole(rows, features),
        stored((rows, features), F32),
        [pltpu.VMEM((rows, 2 * less), BF16)],
        expert_flops,
        6_000_000,
    )(arrived, weight_up)
    pre_act, hidden, send = call(
        forward_kernel,
        (steps,),
        [
            once(*more_block),
            pl.BlockSpec((2 * more, features), lambda step: (step + 1, 0)),
            far,
            far,
        ],
        [whole(rows, features), whole(rows, features), whole(*narrow_block)],
        [stored((rows, features), F32), stored((rows, features), BF16), stored(narrow_block, BF16)],
        [
            pltpu.VMEM((rows, 2 * more), BF16),
            pltpu.VMEM((rows, features), F32),
            pltpu.VMEM((features, HW), BF16),
            pltpu.SemaphoreType.DMA((2,)),
        ],
        2 * expert_flops,
        10_000_000,
    )(arrived_later, weight_up, pre_act, down_cond)
    added = exchange(send)
    offset, noisy = lax.cond(core == 1, of_draws, lambda: early)
    slope = gelu_slope(pre_act)

    delta, send = call(
        head_kernel,
        (1,),
        [
            whole(*narrow_block),
            whole(tok_rows, HW),
            far,
            whole(*noisy.shape),
            far,
            whole(1, HW),
            far,
            far,
        ],
        [whole(tok_rows, HW), whole(*grads_block)],
        [stored((tok_rows, HW), BF16), stored(grads_block, BF16)],
        [
            pltpu.VMEM((tok_rows, HW), F32),
            pltpu.VMEM((experts * MAIN, HW), BF16),
            pltpu.VMEM((experts * small_rows, LANES), F32),
            pltpu.VMEM((NOISE, tok_rows, HW), F32),
            pltpu.VMEM(noise_draws.shape, F32),
            pltpu.VMEM(head_out.shape, BF16),
            pltpu.VMEM((slot_rows, tok_rows), F32),
            pltpu.SemaphoreType.DMA((4,)),
        ],
        1_500_000_000,
        5_000_000,
    )(added, direct, offset, noisy, noise_draws, head_gain.reshape(1, HW), head_out, gate)
    arrived = exchange(send)

    slot_grads, held, small, send = call(
        backward_kernel,
        (steps,),
        [
            once(*grads_block),
            far,
            once(rows, features),
            pl.BlockSpec((2 * half, features), lambda step: (step, 0)),
        ],
        [whole(rows, HW), whole(rows, features), whole(small_rows, LANES), whole(*half_block)],
        [
            stored((rows, HW), BF16),
            stored((rows, features), BF16),
            stored((small_rows, LANES), F32),
            stored(half_block, BF16),
        ],
        [
            pltpu.VMEM((experts * REST, half), F32),
            pltpu.VMEM((features, HW), BF16),
            pltpu.SemaphoreType.DMA,
        ],
        2 * expert_flops,
        10_000_000,
    )(arrived, down_cond, slope, weight_up)
    slot_grads, held, small, send = lax.optimization_barrier((slot_grads, held, small, send))
    front = exchange(send)
    send = call(
        second_kernel,
        (steps,),
        [once(rows, features), pl.BlockSpec((2 * half, features), lambda step: (step + steps, 0))],
        whole(*half_block),
        stored(half_block, BF16),
        [pltpu.VMEM((experts * REST, half), F32)],
        0,
        0,
    )(held, weight_up)

    back = exchange(send)

    block = 512
    cond_grad = call(
        cond_grad_kernel,
        (width // block,),
        [
            once(rows, features),
            once(rows, HW),
            pl.BlockSpec((features, block), lambda step: (0, step)),
            pl.BlockSpec((tok_rows, block), lambda step: (0, step)),
            once(tok_rows, HW),
        ],
        pl.BlockSpec((block, HW), lambda step: (step, 0)),
        stored((width, HW), BF16),
        [pltpu.VMEM((features, HW), BF16)],
        0,
        0,
    )(hidden, slot_grads, weight_down, tokens, delta)
    cond_grad = lax.psum_scatter(cond_grad, DP, scatter_dimension=0, tiled=True).astype(F32)
    cond_grad = lax.psum_scatter(cond_grad, "y", scatter_dimension=0, tiled=True)
    small, front = lax.optimization_barrier((small, front))
    small = lax.all_gather(small, DP, axis=0, tiled=True)
    small = jnp.sum(small.reshape(-1, small_rows, LANES), axis=0)
    high = lax.reduce_precision(small, 8, 7)
    small = jnp.concatenate([high, small - high], axis=0).astype(BF16)
    small = lax.all_gather(small, "y", axis=0, tiled=True)
    ring = lax.axis_size("z")
    cond_grad = cond_grad.astype(BF16).reshape(ring, -1, LANES)
    dense = cond_grad.shape[1]
    sums = jnp.concatenate([cond_grad, jnp.broadcast_to(small[None], (ring,) + small.shape)], axis=1)

    grad_layer = matmul(delta, cond_full, 1, 1)
    scaled_front, mean_front = call(
        front_kernel,
        (1,),
        [whole(*half_block), whole(slot_rows, tok_rows), whole(tok_rows, width), whole(1, width)],
        [whole(tok_rows, WIDE * half), whole(tok_rows, 1)],
        [shaped((tok_rows, WIDE * half), F32), shaped((tok_rows, 1), F32)],
        [],
        1_000_000_000,
        6_000_000,
    )(front, gate, tokens, gain_row)
    input_grad = call(
        finish_kernel,
        (1,),
        [
            whole(*half_block),
            whole(tok_rows, WIDE * half),
            whole(tok_rows, 1),
            whole(slot_rows, tok_rows),
            whole(tok_rows, width),
            whole(tok_rows, width),
            whole(tok_rows, 1),
            whole(1, width),
        ],
        whole(tok_rows, width),
        shaped((tok_rows, width), BF16),
        [pltpu.VMEM((tok_rows, WIDE * half), F32)],
        1_000_000_000,
        8_000_000,
    )(back, scaled_front, mean_front, gate, grad_layer, tokens, inverse, gain_row)
    sums = lax.all_to_all(sums, "z", split_axis=0, concat_axis=0, tiled=True)
    cond_grad, entry_grad, exit_grad, gain_grad, loss_sum = call(
        totals_kernel,
        (1,),
        [whole(*sums.shape)],
        [
            whole(*head_cond.shape),
            whole(*head_in.shape),
            whole(*head_out.shape),
            whole(1, HW),
            whole(1, LANES),
        ],
        [
            shaped(head_cond.shape, F32),
            shaped(head_in.shape, F32),
            shaped(head_out.shape, F32),
            shaped((1, HW), F32),
            shaped((1, LANES), F32),
        ],
        [pltpu.VMEM((dense, LANES), F32), pltpu.VMEM((experts * small_rows, LANES), F32)],
        1_000_000,
        1_000_000,
    )(sums)

    mean_loss = loss_sum[0, 0] / (tok_rows * lax.axis_size(EVERY) * NOISE)
    return (input_grad, cond_grad, entry_grad, exit_grad, gain_grad[0], mean_loss)


def solution(mesh):
    shape = (mesh.shape["dp"] // CORES, CORES, mesh.shape["expert"] // RING, RING)
    fine = Mesh(mesh.devices.reshape(shape), EVERY)
    return jax.shard_map(
        on_device,
        mesh=fine,
        in_specs=(
            P(EVERY, None),
            P(),
            P(EVERY, None),
            P(EVERY, None),
            P(EXPERT, None, None),
            P(EXPERT, None, None),
            P(EVERY, None),
            P(),
            P(),
            P(),
            P(None, EVERY),
            P(None, None, EVERY),
            P(None, EVERY),
        ),
        out_specs=(P(EVERY, None), P(EVERY, None), P(), P(), P(), P()),
        check_vma=False,
    )
```
